32 devices in a mesh: cand: 2 (over y), gx: 4 (over z), gy: 2 (over x), wa: 2 (over core).
Axes of the slice: x: 2, y: 2, z: 4, core: 2. Of those that a mesh axis runs over, the one named last changes fastest.
Arguments:
- field: bfloat16 [4, 4, 2, 4, 4, 128, 128], P('wa', 'cand', None, 'gx', None, 'gy'), parts along dimension 1, may hold values from -6 to 6
- active_rows: int32 [4, 4], P('gx'), may hold values from 0 to 128, as said below
- kern: bfloat16 [4, 2, 4, 64, 128], P('wa'), may hold values from -0.25 to 0.25
- target: float32 [4, 64, 64], P('wa'), may hold values from 0 to 3
Outputs:
- design_grad: float32 [4, 8, 128, 128], P('gx', 'cand', 'gy'), parts along dimension 1
- intensity: float32 [4, 128, 64], P('wa', 'cand'), parts along dimension 1
The draws below stay inside these ranges and needn't reach their ends.
There are 2 independent parts, one for each index of `cand`. The reference program is written for one: setup_inputs(seed, part) draws one part's arguments, and reference() takes and returns one part's arrays. A program takes and returns all parts, laid end to end along the dimension named above; an argument that names none is the same for every part. Nothing has to cross between parts.
Inputs may be any that keep to these rules, and one draw needn't show every extreme that they name: `active_rows`: live rows are counted from a tile's first cell row; tiles near the aperture's centre are full and its corners empty.
All inputs are finite; a program needn't handle non-finite values.
Results may differ from the reference program's by a relative error of at most 0.0075.
Values may be sent and summed in bfloat16 or wider, within the bound.
A program may use at most 128 MiB of HBM per device.

```python
import jax
import jax.numpy as jnp
from jax import lax

WL = 4
POL = 2
CELLS = 128
FP = 64
G = 4


def draw_active_rows(key, part):
    index = jnp.arange(G, dtype=jnp.int32)
    centred = 2 * index - (G - 1)
    radius = centred[:, None] * centred[:, None] + centred[None, :] * centred[None, :]
    border = jax.random.randint(key, (G, G), 1, CELLS, dtype=jnp.int32)
    inside = 4 * radius <= G * G
    outside = radius > G * G
    full = jnp.full((G, G), CELLS, jnp.int32)
    empty = jnp.zeros((G, G), jnp.int32)
    return jnp.where(inside, full, jnp.where(outside, empty, border)).astype(jnp.int32)


def level_of(stream_key, dims, cuts, low, top_value):
    factor_of, own = 1.0, jax.random.fold_in(stream_key, 6)
    for dim, shards_of in cuts:
        draws = jnp.exp(jax.random.uniform(jax.random.fold_in(own, dim), (shards_of,), jnp.float32, low / len(cuts), top_value / len(cuts)))
        factor_of = factor_of * jnp.repeat(draws, dims[dim] // shards_of).reshape([-1 if axis == dim else 1 for axis in range(len(dims))])
    return factor_of


def bell_draw(key, shape, scale, bound, shards=(), held_as=jnp.bfloat16):
    loudness = level_of(key, shape, shards, -0.22, 0.18) if shards else 1.0
    drawn = jax.random.normal(key, shape, jnp.float32) * scale * loudness
    return jnp.minimum(jnp.maximum(drawn, -bound), bound).astype(held_as)


def setup_inputs(seed: int = 0, part: int = 0) -> dict:
    key_of = jax.random.split(jax.random.key(seed), 5)
    own_keys = jax.random.split(jax.random.fold_in(key_of[4], part), 5)
    return {
        "field": bell_draw(own_keys[0], (WL, POL, 2, G, G, CELLS, CELLS), 1.0, 6.0, ((0, 2), (3, 4), (5, 2))),
        "active_rows": draw_active_rows(jax.random.fold_in(key_of[4], 71), part),
        "kern": bell_draw(key_of[2], (WL, 2, G, FP, CELLS), (G * CELLS) ** -0.5, 0.25, ((0, 2),)),
        "target": jnp.clip(3.0 * jax.random.uniform(key_of[3], (WL, FP, FP), jnp.float32) ** level_of(key_of[3], (WL, FP, FP), ((0, 2),), -0.2, 0.2), 0.0, 3.0),
    }


def one_wave(masked_wave, kern_wave, target_wave):
    tiles = masked_wave.shape[2]
    side = masked_wave.shape[4]
    width = tiles * side
    stack_real = kern_wave[0].transpose(0, 2, 1).reshape(width, FP)
    stack_imag = kern_wave[1].transpose(0, 2, 1).reshape(width, FP)
    left_real = kern_wave[0].transpose(1, 0, 2).reshape(FP, width).astype(jnp.float32)
    left_imag = kern_wave[1].transpose(1, 0, 2).reshape(FP, width).astype(jnp.float32)
    high = lax.Precision.HIGHEST
    planes = []
    focals = []
    for polar in range(POL):
        plane_real = masked_wave[polar, 0].transpose(0, 2, 1, 3).reshape(width, width)
        plane_imag = masked_wave[polar, 1].transpose(0, 2, 1, 3).reshape(width, width)
        inner_real = jnp.dot(plane_real, stack_real, preferred_element_type=jnp.float32) - jnp.dot(plane_imag, stack_imag, preferred_element_type=jnp.float32)
        inner_imag = jnp.dot(plane_real, stack_imag, preferred_element_type=jnp.float32) + jnp.dot(plane_imag, stack_real, preferred_element_type=jnp.float32)
        focal_real = jnp.dot(left_real, inner_real, precision=high) - jnp.dot(left_imag, inner_imag, precision=high)
        focal_imag = jnp.dot(left_real, inner_imag, precision=high) + jnp.dot(left_imag, inner_real, precision=high)
        planes.append((plane_real, plane_imag))
        focals.append((focal_real, focal_imag))
    inten = jnp.zeros((FP, FP), jnp.float32)
    for focal_real, focal_imag in focals:
        inten = inten + focal_real * focal_real + focal_imag * focal_imag
    excess = inten - target_wave
    partial_value = jnp.zeros((width, width), jnp.float32)
    for polar in range(POL):
        focal_real, focal_imag = focals[polar]
        plane_real, plane_imag = planes[polar]
        source_real = excess * focal_real
        source_imag = excess * focal_imag
        row_real = (jnp.dot(left_real.T, source_real, precision=high) + jnp.dot(left_imag.T, source_imag, precision=high)).astype(jnp.bfloat16)
        row_imag = (jnp.dot(left_real.T, source_imag, precision=high) - jnp.dot(left_imag.T, source_real, precision=high)).astype(jnp.bfloat16)
        back_real = jnp.dot(row_real, stack_real.T, preferred_element_type=jnp.float32) + jnp.dot(row_imag, stack_imag.T, preferred_element_type=jnp.float32)
        back_imag = jnp.dot(row_imag, stack_real.T, preferred_element_type=jnp.float32) - jnp.dot(row_real, stack_imag.T, preferred_element_type=jnp.float32)
        partial_value = partial_value + back_real * plane_real.astype(jnp.float32) + back_imag * plane_imag.astype(jnp.float32)
    return partial_value, inten


def reference(field, active_rows, kern, target):
    tiles = field.shape[3]
    side = field.shape[5]
    cell_rows = jnp.arange(side, dtype=jnp.int32)
    live = cell_rows[None, None, :, None] < active_rows[:, :, None, None]
    masked = jnp.where(live, field, jnp.zeros((), field.dtype)).astype(jnp.bfloat16)

    def step(items):
        return one_wave(items[0], items[1], items[2])

    partials, inten = lax.map(step, (masked, kern, target))
    scale = jnp.float32(tiles * side / FP)
    total = jnp.sum(partials, axis=0) * scale
    total = total.reshape(tiles, side, tiles, side).transpose(0, 2, 1, 3)
    design_grad = 0.5 * (total + total.transpose(1, 0, 3, 2))
    return design_grad, inten
```

```python
import functools

import jax
import jax.numpy as jnp
from jax import lax
from jax.experimental import pallas as pl
from jax.experimental.pallas import tpu as pltpu
from jax.sharding import PartitionSpec as P

MESH = pl.DeviceIdType.MESH
SHARD_ROWS = 16
LANES = 128


def each(count, body):
    if count <= 16:
        for step in range(count):
            body(step)
    else:
        lax.fori_loop(0, count, lambda step, carry: (body(step), carry)[1], 0)


def times_i(value):
    parts = []
    for first in range(0, value.shape[1], LANES):
        part = pltpu.roll(value[:, first : first + LANES], LANES // 2, 1)
        lane = lax.broadcasted_iota(jnp.int32, part.shape, 1)
        parts.append(jnp.where(lane < LANES // 2, -part, part))
    return jnp.concatenate(parts, axis=1)


def kernel(
    nx, ny, field, rows, kern, target, grad, inten,
    plane, weights, fpart, frecv, src, ibuf, pown, ppeer, total, tsend, trecv,
    rs_send, rs_recv, ag_send, ag_recv, in_send, in_recv, wa_send, wa_recv, tr_send, tr_recv,
):
    n = nx * ny
    gx, gy, wa = lax.axis_index("gx"), lax.axis_index("gy"), lax.axis_index("wa")
    me = gx * ny + gy
    waves, pols, _, _, tiles, side_u, side = field.shape
    fp = kern.shape[3]
    per_wave = fp // SHARD_ROWS
    owners = waves * per_wave
    group = side // side_u

    def peer_of(step):
        return lax.rem(me + step + 1, n)

    def place(peer):
        return {"gx": peer // ny, "gy": lax.rem(peer, ny)}

    barrier = pltpu.get_barrier_semaphore()

    def greet(step):
        pl.semaphore_signal(barrier, inc=1, device_id=place(peer_of(step)), device_id_type=MESH)

    each(n - 1, greet)
    pl.semaphore_signal(barrier, inc=1, device_id={"wa": 1 - wa}, device_id_type=MESH)

    def shard_copy(owner, slot):
        return pltpu.make_async_remote_copy(
            src_ref=fpart.at[owner], dst_ref=frecv.at[slot],
            send_sem=rs_send.at[owner], recv_sem=rs_recv.at[slot],
            device_id=place(owner), device_id_type=MESH,
        )

    row_index = lax.broadcasted_iota(jnp.int32, (side_u, side), 0) + gy * side_u
    for l in range(waves):
        for j in range(tiles):
            real, imag = kern[l, 0, j], kern[l, 1, j]
            at = 2 * side * j
            weights[l, :fp, at : at + side] = real
            weights[l, :fp, at + side : at + 2 * side] = -imag
            weights[l, fp:, at : at + side] = imag
            weights[l, fp:, at + side : at + 2 * side] = real
            live = row_index < rows[0, j]
            for s in range(pols):
                for c in range(2):
                    value = field[l, s, c, 0, j].astype(jnp.float32)
                    plane[l, s * side_u : (s + 1) * side_u, at + c * side : at + (c + 1) * side] = jnp.where(
                        live, value, 0.0
                    ).astype(jnp.bfloat16)
        inner = lax.dot_general(
            plane[l], weights[l], (((1,), (1,)), ((), ())), preferred_element_type=jnp.float32
        )
        inner = jnp.concatenate(
            [inner[s * side_u : (s + 1) * side_u] for s in range(pols)], axis=1
        )
        both = []
        for value in (inner, times_i(inner)):
            both += [jnp.where(gy == k, value, 0.0) for k in range(group)]
        both = jnp.concatenate(both, axis=0)
        high = both.astype(jnp.bfloat16)
        low = (both - high.astype(jnp.float32)).astype(jnp.bfloat16)
        own = jnp.concatenate([kern[l, 0, gx], kern[l, 1, gx]], axis=1)
        focal = jnp.dot(own, high, preferred_element_type=jnp.float32) + jnp.dot(
            own, low, preferred_element_type=jnp.float32
        )
        for k in range(per_wave):
            fpart[l * per_wave + k] = focal[k * SHARD_ROWS : (k + 1) * SHARD_ROWS]
        if l == 0:
            pl.semaphore_wait(barrier, n)
        for k in range(per_wave):
            owner = l * per_wave + lax.rem(me + k, per_wave)

            @pl.when(owner != me)
            def _():
                shard_copy(owner, me).start()

    def source_copy(peer, slot):
        return pltpu.make_async_remote_copy(
            src_ref=src.at[slot], dst_ref=src.at[slot],
            send_sem=ag_send.at[peer], recv_sem=ag_recv.at[slot],
            device_id=place(peer), device_id_type=MESH,
        )

    def intensity_copy(peer, slot):
        return pltpu.make_async_remote_copy(
            src_ref=ibuf.at[slot], dst_ref=ibuf.at[slot],
            send_sem=in_send.at[peer], recv_sem=in_recv.at[slot],
            device_id=place(peer), device_id_type=MESH,
        )

    def owned():
        frecv[me] = fpart[me]

        def arrive(step):
            shard_copy(me, peer_of(step)).wait_recv()

        each(n - 1, arrive)
        if n <= 16:
            focal = frecv[0]
            for slot in range(1, n):
                focal = focal + frecv[slot]
        else:
            focal = lax.fori_loop(
                1, n, lambda slot, value: value + frecv[slot], frecv[0]
            )
        square = focal * focal
        bright = square[:, :LANES]
        for s in range(1, pols):
            bright = bright + square[:, s * LANES : (s + 1) * LANES]
        bright = bright + pltpu.roll(bright, LANES // 2, 1)
        first = pl.multiple_of(lax.rem(me, per_wave) * SHARD_ROWS, SHARD_ROWS)
        goal = target[me // per_wave, pl.ds(first, SHARD_ROWS), :]
        excess = bright - jnp.concatenate([goal, goal], axis=1)
        src[me] = (focal * jnp.concatenate([excess] * pols, axis=1)).astype(jnp.bfloat16)
        each(n - 1, lambda step: source_copy(peer_of(step), me).start())
        half = SHARD_ROWS // 2
        lane = lax.broadcasted_iota(jnp.int32, (half, LANES), 1)
        ibuf[me] = jnp.where(lane < LANES // 2, bright[:half], bright[half:])
        each(n - 1, lambda step: intensity_copy(peer_of(step), me).start())

    if n > owners:
        pl.when(me < owners)(owned)
    else:
        owned()

    for l in range(waves):
        for k in range(per_wave):
            owner = l * per_wave + k

            @pl.when(owner != me)
            def _():
                source_copy(owner, owner).wait_recv()

        source = src[l * per_wave : (l + 1) * per_wave].reshape(fp, pols * LANES)
        turned = (-times_i(source.astype(jnp.float32))).astype(jnp.bfloat16)
        own = kern[l, :, gx].reshape(2 * fp, side)
        side_rows = lax.dot_general(
            own, jnp.concatenate([source, turned], axis=0), (((0,), (0,)), ((), ())),
            preferred_element_type=jnp.float32,
        )
        picked = side_rows[:side_u]
        for k in range(1, group):
            picked = jnp.where(gy == k, side_rows[k * side_u : (k + 1) * side_u], picked)
        picked = jnp.concatenate(
            [picked[:, s * LANES : (s + 1) * LANES] for s in range(pols)], axis=0
        ).astype(jnp.bfloat16)
        for j in range(tiles):
            at = 2 * side * j
            back = jnp.dot(
                picked, weights[l, :, at : at + 2 * side], preferred_element_type=jnp.float32
            )
            terms = back * plane[l, :, at : at + 2 * side].astype(jnp.float32)
            terms = terms[:, :side] + terms[:, side:]
            value = terms[:side_u]
            for s in range(1, pols):
                value = value + terms[s * side_u : (s + 1) * side_u]
            if l > 0:
                value = value + total[j]
            if l < waves - 1:
                total[j] = value
            else:
                pown[j] = (value * jnp.float32(tiles * side / fp)).astype(jnp.bfloat16)

    swap = pltpu.make_async_remote_copy(
        src_ref=pown, dst_ref=ppeer, send_sem=wa_send, recv_sem=wa_recv,
        device_id={"wa": 1 - wa}, device_id_type=MESH,
    )
    swap.start()

    for owner in range(owners):
        @pl.when(owner != me)
        def _():
            intensity_copy(owner, owner).wait_recv()

        l, first, half = owner // per_wave, owner % per_wave * SHARD_ROWS, SHARD_ROWS // 2
        value = ibuf[owner]
        inten[l, first : first + half, :] = value[:, : LANES // 2]
        inten[l, first + half : first + 2 * half, :] = value[:, LANES // 2 :]

    swap.wait()

    packs = tsend.shape[2] // side_u
    short = side_u // packs
    for j in range(tiles):
        value = pown[j].astype(jnp.float32) + ppeer[j].astype(jnp.float32)
        total[j] = value
        turned = value.T
        for k in range(ny):
            block = turned[k * side_u : (k + 1) * side_u]
            block = jnp.concatenate(
                [block[g * short : (g + 1) * short] for g in range(packs)], axis=1
            )
            tsend[j * ny + k] = block.astype(jnp.bfloat16)

    def turned_copy(peer, slot):
        return pltpu.make_async_remote_copy(
            src_ref=tsend.at[peer], dst_ref=trecv.at[slot],
            send_sem=tr_send.at[peer], recv_sem=tr_recv.at[slot],
            device_id=place(peer), device_id_type=MESH,
        )

    each(n - 1, lambda step: turned_copy(peer_of(step), me).start())
    trecv[me] = tsend[me]
    each(n - 1, lambda step: turned_copy(me, peer_of(step)).wait_recv())
    for j in range(tiles):
        blocks = [trecv[j * ny + k].astype(jnp.float32) for k in range(ny)]
        lines = [
            jnp.concatenate([block[:, g * side_u : (g + 1) * side_u] for block in blocks], axis=1)
            for g in range(packs)
        ]
        grad[0, j] = 0.5 * (total[j] + jnp.concatenate(lines, axis=0))

    for owner in range(owners):
        @pl.when(owner != me)
        def _():
            shard_copy(owner, me).wait_send()

    def drain_owned():
        each(n - 1, lambda step: source_copy(peer_of(step), me).wait_send())
        each(n - 1, lambda step: intensity_copy(peer_of(step), me).wait_send())

    if n > owners:
        pl.when(me < owners)(drain_owned)
    else:
        drain_owned()
    each(n - 1, lambda step: turned_copy(peer_of(step), me).wait_send())


def on_device(nx, ny, field, active_rows, kern, target):
    waves, pols, _, _, tiles, side_u, side = field.shape
    fp = kern.shape[3]
    n = nx * ny
    owners = waves * (fp // SHARD_ROWS)
    packs = LANES // side_u
    if (side_u // packs) % 16:
        packs = 1
    turned = (n, side_u // packs, side_u * packs)
    dma = pltpu.SemaphoreType.DMA
    vmem = pl.BlockSpec(memory_space=pltpu.VMEM)
    width = pols * LANES
    return pl.pallas_call(
        functools.partial(kernel, nx, ny),
        out_shape=(
            jax.ShapeDtypeStruct((1, tiles, side_u, side), jnp.float32),
            jax.ShapeDtypeStruct((waves, fp, fp), jnp.float32),
        ),
        in_specs=[vmem, pl.BlockSpec(memory_space=pltpu.SMEM), vmem, vmem],
        out_specs=(vmem, vmem),
        scratch_shapes=[
            pltpu.VMEM((waves, pols * side_u, tiles * 2 * side), jnp.bfloat16),
            pltpu.VMEM((waves, 2 * fp, tiles * 2 * side), jnp.bfloat16),
            pltpu.VMEM((owners, SHARD_ROWS, width), jnp.float32),
            pltpu.VMEM((n, SHARD_ROWS, width), jnp.float32),
            pltpu.VMEM((owners, SHARD_ROWS, width), jnp.bfloat16),
            pltpu.VMEM((owners, SHARD_ROWS // 2, LANES), jnp.float32),
            pltpu.VMEM((tiles, side_u, side), jnp.bfloat16),
            pltpu.VMEM((tiles, side_u, side), jnp.bfloat16),
            pltpu.VMEM((tiles, side_u, side), jnp.float32),
            pltpu.VMEM(turned, jnp.bfloat16),
            pltpu.VMEM(turned, jnp.bfloat16),
            dma((owners,)), dma((n,)),
            dma((n,)), dma((owners,)),
            dma((n,)), dma((owners,)),
            dma, dma,
            dma((n,)), dma((n,)),
        ],
        compiler_params=pltpu.CompilerParams(
            collective_id=0, has_side_effects=True, vmem_limit_bytes=40 << 20
        ),
    )(field, active_rows, kern, target)


def solution(mesh):
    placed = (
        P("wa", "cand", None, "gx", None, "gy", None),
        P("gx", None),
        P("wa", None, None, None, None),
        P("wa", None, None),
    )
    return jax.shard_map(
        functools.partial(on_device, mesh.shape["gx"], mesh.shape["gy"]),
        mesh=mesh,
        in_specs=placed,
        out_specs=(P("gx", "cand", "gy", None), P("wa", "cand", None)),
        check_vma=False,
    )
```

```python
import functools

import jax
import jax.numpy as jnp
from jax import lax
from jax.experimental import pallas as pl
from jax.experimental.pallas import tpu as pltpu
from jax.sharding import PartitionSpec as P

MESH = pl.DeviceIdType.MESH
SHARD_ROWS = 16
LANES = 128


def each(count, body):
    if count <= 16:
        for step in range(count):
            body(step)
    else:
        lax.fori_loop(0, count, lambda step, carry: (body(step), carry)[1], 0)


def times_i(value):
    parts = []
    for first in range(0, value.shape[1], LANES):
        part = pltpu.roll(value[:, first : first + LANES], LANES // 2, 1)
        lane = lax.broadcasted_iota(jnp.int32, part.shape, 1)
        parts.append(jnp.where(lane < LANES // 2, -part, part))
    return jnp.concatenate(parts, axis=1)


def kernel(
    nx, ny, field_far, rows, kern_far, target_far, grad, inten,
    field, kern, target, field_in, kern_in, target_in, plane, weights, fpart, frecv, src, ibuf, pown, ppeer, total, tsend, trecv,
    rs_send, rs_recv, ag_send, ag_recv, in_send, in_recv, wa_send, wa_recv, tr_send, tr_recv,
):
    n = nx * ny
    gx, gy, wa = lax.axis_index("gx"), lax.axis_index("gy"), lax.axis_index("wa")
    me = gx * ny + gy
    waves, pols, _, _, tiles, side_u, side = field.shape
    fp = kern.shape[3]
    loads = []
    for l in range(waves):
        loads.append(
            (
                pltpu.make_async_copy(kern_far.at[l], kern.at[l], kern_in.at[l]),
                pltpu.make_async_copy(field_far.at[l], field.at[l], field_in.at[l]),
            )
        )
        for copy in loads[l]:
            copy.start()
    goals = pltpu.make_async_copy(target_far, target, target_in)
    goals.start()
    per_wave = fp // SHARD_ROWS
    owners = waves * per_wave
    group = side // side_u

    def peer_of(step):
        return lax.rem(me + step + 1, n)

    def place(peer):
        return {"gx": peer // ny, "gy": lax.rem(peer, ny)}

    barrier = pltpu.get_barrier_semaphore()

    def greet(step):
        pl.semaphore_signal(barrier, inc=1, device_id=place(peer_of(step)), device_id_type=MESH)

    each(n - 1, greet)
    pl.semaphore_signal(barrier, inc=1, device_id={"wa": 1 - wa}, device_id_type=MESH)

    def shard_copy(owner, slot):
        return pltpu.make_async_remote_copy(
            src_ref=fpart.at[owner], dst_ref=frecv.at[slot],
            send_sem=rs_send.at[owner], recv_sem=rs_recv.at[slot],
            device_id=place(owner), device_id_type=MESH,
        )

    row_index = lax.broadcasted_iota(jnp.int32, (side_u, side), 0) + gy * side_u
    for l in range(waves):
        for copy in loads[l]:
            copy.wait()
        for j in range(tiles):
            real, imag = kern[l, 0, j], kern[l, 1, j]
            at = 2 * side * j
            weights[l, :fp, at : at + side] = real
            weights[l, :fp, at + side : at + 2 * side] = -imag
            weights[l, fp:, at : at + side] = imag
            weights[l, fp:, at + side : at + 2 * side] = real
            live = row_index < rows[0, j]
            for s in range(pols):
                for c in range(2):
                    value = field[l, s, c, 0, j].astype(jnp.float32)
                    plane[l, s * side_u : (s + 1) * side_u, at + c * side : at + (c + 1) * side] = jnp.where(
                        live, value, 0.0
                    ).astype(jnp.bfloat16)
        inner = lax.dot_general(
            plane[l], weights[l], (((1,), (1,)), ((), ())), preferred_element_type=jnp.float32
        )
        inner = jnp.concatenate(
            [inner[s * side_u : (s + 1) * side_u] for s in range(pols)], axis=1
        )
        both = []
        for value in (inner, times_i(inner)):
            both += [jnp.where(gy == k, value, 0.0) for k in range(group)]
        both = jnp.concatenate(both, axis=0)
        high = both.astype(jnp.bfloat16)
        low = (both - high.astype(jnp.float32)).astype(jnp.bfloat16)
        own = jnp.concatenate([kern[l, 0, gx], kern[l, 1, gx]], axis=1)
        focal = jnp.dot(own, high, preferred_element_type=jnp.float32) + jnp.dot(
            own, low, preferred_element_type=jnp.float32
        )
        for k in range(per_wave):
            fpart[l * per_wave + k] = focal[k * SHARD_ROWS : (k + 1) * SHARD_ROWS]
        if l == 0:
            pl.semaphore_wait(barrier, n)
        for k in range(per_wave):
            owner = l * per_wave + lax.rem(me + k, per_wave)

            @pl.when(owner != me)
            def _():
                shard_copy(owner, me).start()

    goals.wait()

    def source_copy(peer, slot):
        return pltpu.make_async_remote_copy(
            src_ref=src.at[slot], dst_ref=src.at[slot],
            send_sem=ag_send.at[peer], recv_sem=ag_recv.at[slot],
            device_id=place(peer), device_id_type=MESH,
        )

    def intensity_copy(peer, slot):
        return pltpu.make_async_remote_copy(
            src_ref=ibuf.at[slot], dst_ref=ibuf.at[slot],
            send_sem=in_send.at[peer], recv_sem=in_recv.at[slot],
            device_id=place(peer), device_id_type=MESH,
        )

    def owned():
        frecv[me] = fpart[me]

        def arrive(step):
            shard_copy(me, peer_of(step)).wait_recv()

        each(n - 1, arrive)
        if n <= 16:
            focal = frecv[0]
            for slot in range(1, n):
                focal = focal + frecv[slot]
        else:
            focal = lax.fori_loop(
                1, n, lambda slot, value: value + frecv[slot], frecv[0]
            )
        square = focal * focal
        bright = square[:, :LANES]
        for s in range(1, pols):
            bright = bright + square[:, s * LANES : (s + 1) * LANES]
        bright = bright + pltpu.roll(bright, LANES // 2, 1)
        first = pl.multiple_of(lax.rem(me, per_wave) * SHARD_ROWS, SHARD_ROWS)
        goal = target[me // per_wave, pl.ds(first, SHARD_ROWS), :]
        excess = bright - jnp.concatenate([goal, goal], axis=1)
        src[me] = (focal * jnp.concatenate([excess] * pols, axis=1)).astype(jnp.bfloat16)
        each(n - 1, lambda step: source_copy(peer_of(step), me).start())
        half = SHARD_ROWS // 2
        lane = lax.broadcasted_iota(jnp.int32, (half, LANES), 1)
        ibuf[me] = jnp.where(lane < LANES // 2, bright[:half], bright[half:])
        each(n - 1, lambda step: intensity_copy(peer_of(step), me).start())

    if n > owners:
        pl.when(me < owners)(owned)
    else:
        owned()

    def swap(tile):
        return pltpu.make_async_remote_copy(
            src_ref=pown.at[tile], dst_ref=ppeer.at[tile],
            send_sem=wa_send.at[tile], recv_sem=wa_recv.at[tile],
            device_id={"wa": 1 - wa}, device_id_type=MESH,
        )

    for l in range(waves):
        for k in range(per_wave):
            owner = l * per_wave + k

            @pl.when(owner != me)
            def _():
                source_copy(owner, owner).wait_recv()

        source = src[l * per_wave : (l + 1) * per_wave].reshape(fp, pols * LANES)
        turned = (-times_i(source.astype(jnp.float32))).astype(jnp.bfloat16)
        own = kern[l, :, gx].reshape(2 * fp, side)
        side_rows = lax.dot_general(
            own, jnp.concatenate([source, turned], axis=0), (((0,), (0,)), ((), ())),
            preferred_element_type=jnp.float32,
        )
        picked = side_rows[:side_u]
        for k in range(1, group):
            picked = jnp.where(gy == k, side_rows[k * side_u : (k + 1) * side_u], picked)
        picked = jnp.concatenate(
            [picked[:, s * LANES : (s + 1) * LANES] for s in range(pols)], axis=0
        ).astype(jnp.bfloat16)
        for j in range(tiles):
            at = 2 * side * j
            back = jnp.dot(
                picked, weights[l, :, at : at + 2 * side], preferred_element_type=jnp.float32
            )
            terms = back * plane[l, :, at : at + 2 * side].astype(jnp.float32)
            terms = terms[:, :side] + terms[:, side:]
            value = terms[:side_u]
            for s in range(1, pols):
                value = value + terms[s * side_u : (s + 1) * side_u]
            if l > 0:
                value = value + total[j]
            if l < waves - 1:
                total[j] = value
            else:
                pown[j] = (value * jnp.float32(tiles * side / fp)).astype(jnp.bfloat16)
                swap(j).start()

    packs = tsend.shape[2] // side_u
    short = side_u // packs

    def turned_copy(peer, slot):
        return pltpu.make_async_remote_copy(
            src_ref=tsend.at[peer], dst_ref=trecv.at[slot],
            send_sem=tr_send.at[peer], recv_sem=tr_recv.at[slot],
            device_id=place(peer), device_id_type=MESH,
        )

    def turn(step):
        tile = lax.rem(gx + 1 + step, tiles)
        swap(tile).wait_recv()
        value = pown[tile].astype(jnp.float32) + ppeer[tile].astype(jnp.float32)
        total[tile] = value
        turned = value.T
        for k in range(ny):
            block = turned[k * side_u : (k + 1) * side_u]
            block = jnp.concatenate(
                [block[g * short : (g + 1) * short] for g in range(packs)], axis=1
            )
            peer = tile * ny + k
            tsend[peer] = block.astype(jnp.bfloat16)

            @pl.when(peer != me)
            def _():
                turned_copy(peer, me).start()

    each(tiles, turn)

    for owner in range(owners):
        @pl.when(owner != me)
        def _():
            intensity_copy(owner, owner).wait_recv()

        l, first, half = owner // per_wave, owner % per_wave * SHARD_ROWS, SHARD_ROWS // 2
        value = ibuf[owner]
        inten[l, first : first + half, :] = value[:, : LANES // 2]
        inten[l, first + half : first + 2 * half, :] = value[:, LANES // 2 :]

    trecv[me] = tsend[me]
    each(n - 1, lambda step: turned_copy(me, peer_of(step)).wait_recv())
    for j in range(tiles):
        blocks = [trecv[j * ny + k].astype(jnp.float32) for k in range(ny)]
        lines = [
            jnp.concatenate([block[:, g * side_u : (g + 1) * side_u] for block in blocks], axis=1)
            for g in range(packs)
        ]
        grad[0, j] = 0.5 * (total[j] + jnp.concatenate(lines, axis=0))

    each(tiles, lambda tile: swap(tile).wait_send())
    for owner in range(owners):
        @pl.when(owner != me)
        def _():
            shard_copy(owner, me).wait_send()

    def drain_owned():
        each(n - 1, lambda step: source_copy(peer_of(step), me).wait_send())
        each(n - 1, lambda step: intensity_copy(peer_of(step), me).wait_send())

    if n > owners:
        pl.when(me < owners)(drain_owned)
    else:
        drain_owned()
    each(n - 1, lambda step: turned_copy(peer_of(step), me).wait_send())


def on_device(nx, ny, field, active_rows, kern, target):
    waves, pols, _, _, tiles, side_u, side = field.shape
    fp = kern.shape[3]
    n = nx * ny
    owners = waves * (fp // SHARD_ROWS)
    packs = LANES // side_u
    if (side_u // packs) % 16:
        packs = 1
    turned = (n, side_u // packs, side_u * packs)
    dma = pltpu.SemaphoreType.DMA
    vmem = pl.BlockSpec(memory_space=pltpu.VMEM)
    far = pl.BlockSpec(memory_space=pltpu.HBM)
    width = pols * LANES
    return pl.pallas_call(
        functools.partial(kernel, nx, ny),
        out_shape=(
            jax.ShapeDtypeStruct((1, tiles, side_u, side), jnp.float32),
            jax.ShapeDtypeStruct((waves, fp, fp), jnp.float32),
        ),
        in_specs=[far, pl.BlockSpec(memory_space=pltpu.SMEM), far, far],
        out_specs=(vmem, vmem),
        scratch_shapes=[
            pltpu.VMEM(field.shape, field.dtype),
            pltpu.VMEM(kern.shape, kern.dtype),
            pltpu.VMEM(target.shape, target.dtype),
            dma((waves,)), dma((waves,)), dma,
            pltpu.VMEM((waves, pols * side_u, tiles * 2 * side), jnp.bfloat16),
            pltpu.VMEM((waves, 2 * fp, tiles * 2 * side), jnp.bfloat16),
            pltpu.VMEM((owners, SHARD_ROWS, width), jnp.float32),
            pltpu.VMEM((n, SHARD_ROWS, width), jnp.float32),
            pltpu.VMEM((owners, SHARD_ROWS, width), jnp.bfloat16),
            pltpu.VMEM((owners, SHARD_ROWS // 2, LANES), jnp.float32),
            pltpu.VMEM((tiles, side_u, side), jnp.bfloat16),
            pltpu.VMEM((tiles, side_u, side), jnp.bfloat16),
            pltpu.VMEM((tiles, side_u, side), jnp.float32),
            pltpu.VMEM(turned, jnp.bfloat16),
            pltpu.VMEM(turned, jnp.bfloat16),
            dma((owners,)), dma((n,)),
            dma((n,)), dma((owners,)),
            dma((n,)), dma((owners,)),
            dma((tiles,)), dma((tiles,)),
            dma((n,)), dma((n,)),
        ],
        compiler_params=pltpu.CompilerParams(
            collective_id=0, has_side_effects=True, vmem_limit_bytes=40 << 20
        ),
    )(field, active_rows, kern, target)


def solution(mesh):
    placed = (
        P("wa", "cand", None, "gx", None, "gy", None),
        P("gx", None),
        P("wa", None, None, None, None),
        P("wa", None, None),
    )
    return jax.shard_map(
        functools.partial(on_device, mesh.shape["gx"], mesh.shape["gy"]),
        mesh=mesh,
        in_specs=placed,
        out_specs=(P("gx", "cand", "gy", None), P("wa", "cand", None)),
        check_vma=False,
    )
```

```python
import functools

import jax
import jax.numpy as jnp
from jax import lax
from jax.experimental import pallas as pl
from jax.experimental.pallas import tpu as pltpu
from jax.sharding import PartitionSpec as P

MESH = pl.DeviceIdType.MESH
SHARD_ROWS = 16
LANES = 128


def each(count, body):
    if count <= 16:
        for step in range(count):
            body(step)
    else:
        lax.fori_loop(0, count, lambda step, carry: (body(step), carry)[1], 0)


def times_i(value):
    parts = []
    for first in range(0, value.shape[1], LANES):
        part = pltpu.roll(value[:, first : first + LANES], LANES // 2, 1)
        lane = lax.broadcasted_iota(jnp.int32, part.shape, 1)
        parts.append(jnp.where(lane < LANES // 2, -part, part))
    return jnp.concatenate(parts, axis=1)


def kernel(
    nx, ny, field_far, rows, kern_far, target_far, grad, inten,
    field, kern, target, field_in, kern_in, target_in, plane, weights, fpart, frecv, src, ibuf, pown, ppeer, total, tsend, trecv,
    rs_send, rs_recv, ag_send, ag_recv, in_send, in_recv, wa_send, wa_recv, tr_send, tr_recv,
):
    n = nx * ny
    gx, gy, wa = lax.axis_index("gx"), lax.axis_index("gy"), lax.axis_index("wa")
    me = gx * ny + gy
    waves, pols, _, _, tiles, side_u, side = field.shape
    fp = kern.shape[3]
    loads = []
    for l in range(waves):
        loads.append(
            (
                pltpu.make_async_copy(kern_far.at[l], kern.at[l], kern_in.at[l]),
                pltpu.make_async_copy(field_far.at[l], field.at[l], field_in.at[l]),
            )
        )
        for copy in loads[l]:
            copy.start()
    goals = pltpu.make_async_copy(target_far, target, target_in)
    goals.start()
    per_wave = fp // SHARD_ROWS
    owners = waves * per_wave
    group = side // side_u

    def peer_of(step):
        return lax.rem(me + step + 1, n)

    def place(peer):
        return {"gx": peer // ny, "gy": lax.rem(peer, ny)}

    barrier = pltpu.get_barrier_semaphore()

    def greet(step):
        pl.semaphore_signal(barrier, inc=1, device_id=place(peer_of(step)), device_id_type=MESH)

    each(n - 1, greet)
    pl.semaphore_signal(barrier, inc=1, device_id={"wa": 1 - wa}, device_id_type=MESH)

    def shard_copy(owner, slot):
        return pltpu.make_async_remote_copy(
            src_ref=fpart.at[owner], dst_ref=frecv.at[slot],
            send_sem=rs_send.at[owner], recv_sem=rs_recv.at[slot],
            device_id=place(owner), device_id_type=MESH,
        )

    row_index = lax.broadcasted_iota(jnp.int32, (side_u, side), 0) + gy * side_u
    for l in range(waves):
        for copy in loads[l]:
            copy.wait()
        for j in range(tiles):
            real, imag = kern[l, 0, j], kern[l, 1, j]
            at = 2 * side * j
            weights[l, :fp, at : at + side] = real
            weights[l, :fp, at + side : at + 2 * side] = -imag
            weights[l, fp:, at : at + side] = imag
            weights[l, fp:, at + side : at + 2 * side] = real
            live = row_index < rows[0, j]
            for s in range(pols):
                for c in range(2):
                    value = field[l, s, c, 0, j].astype(jnp.float32)
                    plane[l, s * side_u : (s + 1) * side_u, at + c * side : at + (c + 1) * side] = jnp.where(
                        live, value, 0.0
                    ).astype(jnp.bfloat16)
        inner = lax.dot_general(
            plane[l], weights[l], (((1,), (1,)), ((), ())), preferred_element_type=jnp.float32
        )
        inner = jnp.concatenate(
            [inner[s * side_u : (s + 1) * side_u] for s in range(pols)], axis=1
        )
        both = []
        for value in (inner, times_i(inner)):
            both += [jnp.where(gy == k, value, 0.0) for k in range(group)]
        both = jnp.concatenate(both, axis=0)
        high = both.astype(jnp.bfloat16)
        low = (both - high.astype(jnp.float32)).astype(jnp.bfloat16)
        own = jnp.concatenate([kern[l, 0, gx], kern[l, 1, gx]], axis=1)
        focal = jnp.dot(own, high, preferred_element_type=jnp.float32) + jnp.dot(
            own, low, preferred_element_type=jnp.float32
        )
        for k in range(per_wave):
            fpart[l * per_wave + k] = focal[k * SHARD_ROWS : (k + 1) * SHARD_ROWS]
        if l == 0:
            pl.semaphore_wait(barrier, n)
        for k in range(per_wave):
            owner = l * per_wave + lax.rem(me + k, per_wave)

            @pl.when(owner != me)
            def _():
                shard_copy(owner, me).start()

    goals.wait()

    def source_copy(peer, slot):
        return pltpu.make_async_remote_copy(
            src_ref=src.at[slot], dst_ref=src.at[slot],
            send_sem=ag_send.at[peer], recv_sem=ag_recv.at[slot],
            device_id=place(peer), device_id_type=MESH,
        )

    def intensity_copy(peer, slot):
        return pltpu.make_async_remote_copy(
            src_ref=ibuf.at[slot], dst_ref=ibuf.at[slot],
            send_sem=in_send.at[peer], recv_sem=in_recv.at[slot],
            device_id=place(peer), device_id_type=MESH,
        )

    def owned():
        frecv[me] = fpart[me]

        def arrive(step):
            shard_copy(me, peer_of(step)).wait_recv()

        each(n - 1, arrive)
        if n <= 16:
            focal = frecv[0]
            for slot in range(1, n):
                focal = focal + frecv[slot]
        else:
            focal = lax.fori_loop(
                1, n, lambda slot, value: value + frecv[slot], frecv[0]
            )
        square = focal * focal
        bright = square[:, :LANES]
        for s in range(1, pols):
            bright = bright + square[:, s * LANES : (s + 1) * LANES]
        bright = bright + pltpu.roll(bright, LANES // 2, 1)
        first = pl.multiple_of(lax.rem(me, per_wave) * SHARD_ROWS, SHARD_ROWS)
        goal = target[me // per_wave, pl.ds(first, SHARD_ROWS), :]
        excess = bright - jnp.concatenate([goal, goal], axis=1)
        src[me] = (focal * jnp.concatenate([excess] * pols, axis=1)).astype(jnp.bfloat16)
        each(n - 1, lambda step: source_copy(peer_of(step), me).start())
        half = SHARD_ROWS // 2
        lane = lax.broadcasted_iota(jnp.int32, (half, LANES), 1)
        ibuf[me] = jnp.where(lane < LANES // 2, bright[:half], bright[half:])
        each(n - 1, lambda step: intensity_copy(peer_of(step), me).start())

    if n > owners:
        pl.when(me < owners)(owned)
    else:
        owned()

    def swap(tile):
        return pltpu.make_async_remote_copy(
            src_ref=pown.at[tile], dst_ref=ppeer.at[tile],
            send_sem=wa_send.at[tile], recv_sem=wa_recv.at[tile],
            device_id={"wa": 1 - wa}, device_id_type=MESH,
        )

    for l in range(waves):
        for k in range(per_wave):
            owner = l * per_wave + k

            @pl.when(owner != me)
            def _():
                source_copy(owner, owner).wait_recv()

        source = src[l * per_wave : (l + 1) * per_wave].reshape(fp, pols * LANES)
        turned = (-times_i(source.astype(jnp.float32))).astype(jnp.bfloat16)
        own = kern[l, :, gx].reshape(2 * fp, side)
        side_rows = lax.dot_general(
            own, jnp.concatenate([source, turned], axis=0), (((0,), (0,)), ((), ())),
            preferred_element_type=jnp.float32,
        )
        picked = side_rows[:side_u]
        for k in range(1, group):
            picked = jnp.where(gy == k, side_rows[k * side_u : (k + 1) * side_u], picked)
        picked = jnp.concatenate(
            [picked[:, s * LANES : (s + 1) * LANES] for s in range(pols)], axis=0
        ).astype(jnp.bfloat16)
        for j in range(tiles):
            at = 2 * side * j
            back = jnp.dot(
                picked, weights[l, :, at : at + 2 * side], preferred_element_type=jnp.float32
            )
            terms = back * plane[l, :, at : at + 2 * side].astype(jnp.float32)
            terms = terms[:, :side] + terms[:, side:]
            value = terms[:side_u]
            for s in range(1, pols):
                value = value + terms[s * side_u : (s + 1) * side_u]
            if l > 0:
                value = value + total[j]
            if l < waves - 1:
                total[j] = value
            else:
                pown[j] = (value * jnp.float32(tiles * side / fp)).astype(jnp.bfloat16)
                swap(j).start()

    packs = tsend.shape[2] // side_u
    short = side_u // packs

    def turned_copy(peer, slot):
        return pltpu.make_async_remote_copy(
            src_ref=tsend.at[peer], dst_ref=trecv.at[slot],
            send_sem=tr_send.at[peer], recv_sem=tr_recv.at[slot],
            device_id=place(peer), device_id_type=MESH,
        )

    def turn(step):
        tile = lax.rem(gx + 1 + step, tiles)
        swap(tile).wait_recv()
        value = pown[tile].astype(jnp.float32) + ppeer[tile].astype(jnp.float32)
        total[tile] = value
        turned = value.T
        for k in range(ny):
            block = turned[k * side_u : (k + 1) * side_u]
            block = jnp.concatenate(
                [block[g * short : (g + 1) * short] for g in range(packs)], axis=1
            )
            peer = tile * ny + k
            tsend[peer] = block.astype(jnp.bfloat16)

            @pl.when(peer != me)
            def _():
                turned_copy(peer, me).start()

    each(tiles, turn)

    for owner in range(owners):
        @pl.when(owner != me)
        def _():
            intensity_copy(owner, owner).wait_recv()

        l, first, half = owner // per_wave, owner % per_wave * SHARD_ROWS, SHARD_ROWS // 2
        value = ibuf[owner]
        inten[l, first : first + half, :] = value[:, : LANES // 2]
        inten[l, first + half : first + 2 * half, :] = value[:, LANES // 2 :]

    trecv[me] = tsend[me]
    each(n - 1, lambda step: turned_copy(me, peer_of(step)).wait_recv())
    for j in range(tiles):
        blocks = [trecv[j * ny + k].astype(jnp.float32) for k in range(ny)]
        lines = [
            jnp.concatenate([block[:, g * side_u : (g + 1) * side_u] for block in blocks], axis=1)
            for g in range(packs)
        ]
        grad[0, j] = 0.5 * (total[j] + jnp.concatenate(lines, axis=0))

    each(tiles, lambda tile: swap(tile).wait_send())
    for owner in range(owners):
        @pl.when(owner != me)
        def _():
            shard_copy(owner, me).wait_send()

    def drain_owned():
        each(n - 1, lambda step: source_copy(peer_of(step), me).wait_send())
        each(n - 1, lambda step: intensity_copy(peer_of(step), me).wait_send())

    if n > owners:
        pl.when(me < owners)(drain_owned)
    else:
        drain_owned()
    each(n - 1, lambda step: turned_copy(peer_of(step), me).wait_send())


def on_device(nx, ny, field, active_rows, kern, target):
    waves, pols, _, _, tiles, side_u, side = field.shape
    fp = kern.shape[3]
    n = nx * ny
    owners = waves * (fp // SHARD_ROWS)
    packs = LANES // side_u
    if (side_u // packs) % 16:
        packs = 1
    turned = (n, side_u // packs, side_u * packs)
    dma = pltpu.SemaphoreType.DMA
    vmem = pl.BlockSpec(memory_space=pltpu.VMEM)
    far = pl.BlockSpec(memory_space=pltpu.HBM)
    width = pols * LANES
    return pl.pallas_call(
        functools.partial(kernel, nx, ny),
        out_shape=(
            jax.ShapeDtypeStruct((1, tiles, side_u, side), jnp.float32),
            jax.ShapeDtypeStruct((waves, fp, fp), jnp.float32),
        ),
        in_specs=[far, pl.BlockSpec(memory_space=pltpu.SMEM), far, far],
        out_specs=(vmem, vmem),
        scratch_shapes=[
            pltpu.VMEM(field.shape, field.dtype),
            pltpu.VMEM(kern.shape, kern.dtype),
            pltpu.VMEM(target.shape, target.dtype),
            dma((waves,)), dma((waves,)), dma,
            pltpu.VMEM((waves, pols * side_u, tiles * 2 * side), jnp.bfloat16),
            pltpu.VMEM((waves, 2 * fp, tiles * 2 * side), jnp.bfloat16),
            pltpu.VMEM((owners, SHARD_ROWS, width), jnp.float32),
            pltpu.VMEM((n, SHARD_ROWS, width), jnp.float32),
            pltpu.VMEM((owners, SHARD_ROWS, width), jnp.bfloat16),
            pltpu.VMEM((owners, SHARD_ROWS // 2, LANES), jnp.float32),
            pltpu.VMEM((tiles, side_u, side), jnp.bfloat16),
            pltpu.VMEM((tiles, side_u, side), jnp.bfloat16),
            pltpu.VMEM((tiles, side_u, side), jnp.float32),
            pltpu.VMEM(turned, jnp.bfloat16),
            pltpu.VMEM(turned, jnp.bfloat16),
            dma((owners,)), dma((n,)),
            dma((n,)), dma((owners,)),
            dma((n,)), dma((owners,)),
            dma((tiles,)), dma((tiles,)),
            dma((n,)), dma((n,)),
        ],
        compiler_params=pltpu.CompilerParams(
            collective_id=0, has_side_effects=True, vmem_limit_bytes=64 << 20
        ),
    )(field, active_rows, kern, target)


def solution(mesh):
    placed = (
        P("wa", "cand", None, "gx", None, "gy", None),
        P("gx", None),
        P("wa", None, None, None, None),
        P("wa", None, None),
    )
    return jax.shard_map(
        functools.partial(on_device, mesh.shape["gx"], mesh.shape["gy"]),
        mesh=mesh,
        in_specs=placed,
        out_specs=(P("gx", "cand", "gy", None), P("wa", "cand", None)),
        check_vma=False,
    )
```

```python
import functools

import jax
import jax.numpy as jnp
from jax import lax
from jax.experimental import pallas as pl
from jax.experimental.pallas import tpu as pltpu
from jax.sharding import PartitionSpec as P

MESH = pl.DeviceIdType.MESH
SHARD_ROWS = 16
LANES = 128


def each(count, body):
    if count <= 16:
        for step in range(count):
            body(step)
    else:
        lax.fori_loop(0, count, lambda step, carry: (body(step), carry)[1], 0)


def times_i(value):
    parts = []
    for first in range(0, value.shape[1], LANES):
        part = pltpu.roll(value[:, first : first + LANES], LANES // 2, 1)
        lane = lax.broadcasted_iota(jnp.int32, part.shape, 1)
        parts.append(jnp.where(lane < LANES // 2, -part, part))
    return jnp.concatenate(parts, axis=1)


def kernel(
    nx, ny, field_far, rows, kern_far, target_far, grad, inten,
    field, kern, target, field_in, kern_in, target_in, plane, weights, fpart, frecv, src, ibuf, pown, ppeer, total, tsend, trecv,
    rs_send, rs_recv, ag_send, ag_recv, in_send, in_recv, wa_send, wa_recv, tr_send, tr_recv,
):
    n = nx * ny
    gx, gy, wa = lax.axis_index("gx"), lax.axis_index("gy"), lax.axis_index("wa")
    me = gx * ny + gy
    waves, pols, _, _, tiles, side_u, side = field.shape
    fp = kern.shape[3]
    loads = []
    for l in range(waves):
        loads.append(
            (
                pltpu.make_async_copy(kern_far.at[l], kern.at[l], kern_in.at[l]),
                pltpu.make_async_copy(field_far.at[l], field.at[l], field_in.at[l]),
            )
        )
        for copy in loads[l]:
            copy.start()
    goals = pltpu.make_async_copy(target_far, target, target_in)
    goals.start()
    per_wave = fp // SHARD_ROWS
    owners = waves * per_wave
    group = side // side_u

    def peer_of(step):
        return lax.rem(me + step + 1, n)

    def place(peer):
        return {"gx": peer // ny, "gy": lax.rem(peer, ny)}

    barrier = pltpu.get_barrier_semaphore()

    def greet(step):
        pl.semaphore_signal(barrier, inc=1, device_id=place(peer_of(step)), device_id_type=MESH)

    each(n - 1, greet)
    pl.semaphore_signal(barrier, inc=1, device_id={"wa": 1 - wa}, device_id_type=MESH)

    def shard_copy(owner, slot):
        return pltpu.make_async_remote_copy(
            src_ref=fpart.at[owner], dst_ref=frecv.at[slot],
            send_sem=rs_send.at[owner], recv_sem=rs_recv.at[slot],
            device_id=place(owner), device_id_type=MESH,
        )

    row_index = lax.broadcasted_iota(jnp.int32, (side_u, side), 0) + gy * side_u
    for l in range(waves):
        for copy in loads[l]:
            copy.wait()
        for j in range(tiles):
            real, imag = kern[l, 0, j], kern[l, 1, j]
            at = 2 * side * j
            weights[l, :fp, at : at + side] = real
            weights[l, :fp, at + side : at + 2 * side] = -imag
            weights[l, fp:, at : at + side] = imag
            weights[l, fp:, at + side : at + 2 * side] = real
            live = row_index < rows[0, j]
            for s in range(pols):
                for c in range(2):
                    value = field[l, s, c, 0, j].astype(jnp.float32)
                    plane[l, s * side_u : (s + 1) * side_u, at + c * side : at + (c + 1) * side] = jnp.where(
                        live, value, 0.0
                    ).astype(jnp.bfloat16)
        inner = lax.dot_general(
            plane[l], weights[l], (((1,), (1,)), ((), ())), preferred_element_type=jnp.float32
        )
        inner = jnp.concatenate(
            [inner[s * side_u : (s + 1) * side_u] for s in range(pols)], axis=1
        )
        both = []
        for value in (inner, times_i(inner)):
            both += [jnp.where(gy == k, value, 0.0) for k in range(group)]
        both = jnp.concatenate(both, axis=0)
        high = both.astype(jnp.bfloat16)
        low = (both - high.astype(jnp.float32)).astype(jnp.bfloat16)
        own = jnp.concatenate([kern[l, 0, gx], kern[l, 1, gx]], axis=1)
        focal = jnp.dot(own, high, preferred_element_type=jnp.float32) + jnp.dot(
            own, low, preferred_element_type=jnp.float32
        )
        for k in range(per_wave):
            fpart[l * per_wave + k] = focal[k * SHARD_ROWS : (k + 1) * SHARD_ROWS].astype(
                jnp.bfloat16
            )
        if l == 0:
            pl.semaphore_wait(barrier, n)
        for k in range(per_wave):
            owner = l * per_wave + lax.rem(me + k, per_wave)

            @pl.when(owner != me)
            def _():
                shard_copy(owner, me).start()

    goals.wait()

    def source_copy(peer, slot):
        return pltpu.make_async_remote_copy(
            src_ref=src.at[slot], dst_ref=src.at[slot],
            send_sem=ag_send.at[peer], recv_sem=ag_recv.at[slot],
            device_id=place(peer), device_id_type=MESH,
        )

    def intensity_copy(peer, slot):
        return pltpu.make_async_remote_copy(
            src_ref=ibuf.at[slot], dst_ref=ibuf.at[slot],
            send_sem=in_send.at[peer], recv_sem=in_recv.at[slot],
            device_id=place(peer), device_id_type=MESH,
        )

    def owned():
        frecv[me] = fpart[me]

        def arrive(step):
            shard_copy(me, peer_of(step)).wait_recv()

        each(n - 1, arrive)
        if n <= 16:
            focal = frecv[0].astype(jnp.float32)
            for slot in range(1, n):
                focal = focal + frecv[slot].astype(jnp.float32)
        else:
            focal = lax.fori_loop(
                1, n, lambda slot, value: value + frecv[slot].astype(jnp.float32),
                frecv[0].astype(jnp.float32),
            )
        square = focal * focal
        bright = square[:, :LANES]
        for s in range(1, pols):
            bright = bright + square[:, s * LANES : (s + 1) * LANES]
        bright = bright + pltpu.roll(bright, LANES // 2, 1)
        first = pl.multiple_of(lax.rem(me, per_wave) * SHARD_ROWS, SHARD_ROWS)
        goal = target[me // per_wave, pl.ds(first, SHARD_ROWS), :]
        excess = bright - jnp.concatenate([goal, goal], axis=1)
        src[me] = (focal * jnp.concatenate([excess] * pols, axis=1)).astype(jnp.bfloat16)
        each(n - 1, lambda step: source_copy(peer_of(step), me).start())
        half = SHARD_ROWS // 2
        lane = lax.broadcasted_iota(jnp.int32, (half, LANES), 1)
        ibuf[me] = jnp.where(lane < LANES // 2, bright[:half], bright[half:])
        each(n - 1, lambda step: intensity_copy(peer_of(step), me).start())

    if n > owners:
        pl.when(me < owners)(owned)
    else:
        owned()

    def swap(tile):
        return pltpu.make_async_remote_copy(
            src_ref=pown.at[tile], dst_ref=ppeer.at[tile],
            send_sem=wa_send.at[tile], recv_sem=wa_recv.at[tile],
            device_id={"wa": 1 - wa}, device_id_type=MESH,
        )

    for l in range(waves):
        for k in range(per_wave):
            owner = l * per_wave + k

            @pl.when(owner != me)
            def _():
                source_copy(owner, owner).wait_recv()

        source = src[l * per_wave : (l + 1) * per_wave].reshape(fp, pols * LANES)
        turned = (-times_i(source.astype(jnp.float32))).astype(jnp.bfloat16)
        own = kern[l, :, gx].reshape(2 * fp, side)
        side_rows = lax.dot_general(
            own, jnp.concatenate([source, turned], axis=0), (((0,), (0,)), ((), ())),
            preferred_element_type=jnp.float32,
        )
        picked = side_rows[:side_u]
        for k in range(1, group):
            picked = jnp.where(gy == k, side_rows[k * side_u : (k + 1) * side_u], picked)
        picked = jnp.concatenate(
            [picked[:, s * LANES : (s + 1) * LANES] for s in range(pols)], axis=0
        ).astype(jnp.bfloat16)
        for j in range(tiles):
            at = 2 * side * j
            back = jnp.dot(
                picked, weights[l, :, at : at + 2 * side], preferred_element_type=jnp.float32
            )
            terms = back * plane[l, :, at : at + 2 * side].astype(jnp.float32)
            terms = terms[:, :side] + terms[:, side:]
            value = terms[:side_u]
            for s in range(1, pols):
                value = value + terms[s * side_u : (s + 1) * side_u]
            if l > 0:
                value = value + total[j]
            if l < waves - 1:
                total[j] = value
            else:
                pown[j] = (value * jnp.float32(tiles * side / fp)).astype(jnp.bfloat16)
                swap(j).start()

    packs = tsend.shape[2] // side_u
    short = side_u // packs

    def turned_copy(peer, slot):
        return pltpu.make_async_remote_copy(
            src_ref=tsend.at[peer], dst_ref=trecv.at[slot],
            send_sem=tr_send.at[peer], recv_sem=tr_recv.at[slot],
            device_id=place(peer), device_id_type=MESH,
        )

    def turn(step):
        tile = lax.rem(gx + 1 + step, tiles)
        swap(tile).wait_recv()
        value = pown[tile].astype(jnp.float32) + ppeer[tile].astype(jnp.float32)
        total[tile] = value
        turned = value.T
        for k in range(ny):
            block = turned[k * side_u : (k + 1) * side_u]
            block = jnp.concatenate(
                [block[g * short : (g + 1) * short] for g in range(packs)], axis=1
            )
            peer = tile * ny + k
            tsend[peer] = block.astype(jnp.bfloat16)

            @pl.when(peer != me)
            def _():
                turned_copy(peer, me).start()

    each(tiles, turn)

    for owner in range(owners):
        @pl.when(owner != me)
        def _():
            intensity_copy(owner, owner).wait_recv()

        l, first, half = owner // per_wave, owner % per_wave * SHARD_ROWS, SHARD_ROWS // 2
        value = ibuf[owner]
        inten[l, first : first + half, :] = value[:, : LANES // 2]
        inten[l, first + half : first + 2 * half, :] = value[:, LANES // 2 :]

    trecv[me] = tsend[me]
    each(n - 1, lambda step: turned_copy(me, peer_of(step)).wait_recv())
    for j in range(tiles):
        blocks = [trecv[j * ny + k].astype(jnp.float32) for k in range(ny)]
        lines = [
            jnp.concatenate([block[:, g * side_u : (g + 1) * side_u] for block in blocks], axis=1)
            for g in range(packs)
        ]
        grad[0, j] = 0.5 * (total[j] + jnp.concatenate(lines, axis=0))

    each(tiles, lambda tile: swap(tile).wait_send())
    for owner in range(owners):
        @pl.when(owner != me)
        def _():
            shard_copy(owner, me).wait_send()

    def drain_owned():
        each(n - 1, lambda step: source_copy(peer_of(step), me).wait_send())
        each(n - 1, lambda step: intensity_copy(peer_of(step), me).wait_send())

    if n > owners:
        pl.when(me < owners)(drain_owned)
    else:
        drain_owned()
    each(n - 1, lambda step: turned_copy(peer_of(step), me).wait_send())


def on_device(nx, ny, field, active_rows, kern, target):
    waves, pols, _, _, tiles, side_u, side = field.shape
    fp = kern.shape[3]
    n = nx * ny
    owners = waves * (fp // SHARD_ROWS)
    packs = LANES // side_u
    if (side_u // packs) % 16:
        packs = 1
    turned = (n, side_u // packs, side_u * packs)
    dma = pltpu.SemaphoreType.DMA
    vmem = pl.BlockSpec(memory_space=pltpu.VMEM)
    far = pl.BlockSpec(memory_space=pltpu.HBM)
    width = pols * LANES
    return pl.pallas_call(
        functools.partial(kernel, nx, ny),
        out_shape=(
            jax.ShapeDtypeStruct((1, tiles, side_u, side), jnp.float32),
            jax.ShapeDtypeStruct((waves, fp, fp), jnp.float32),
        ),
        in_specs=[far, pl.BlockSpec(memory_space=pltpu.SMEM), far, far],
        out_specs=(vmem, vmem),
        scratch_shapes=[
            pltpu.VMEM(field.shape, field.dtype),
            pltpu.VMEM(kern.shape, kern.dtype),
            pltpu.VMEM(target.shape, target.dtype),
            dma((waves,)), dma((waves,)), dma,
            pltpu.VMEM((waves, pols * side_u, tiles * 2 * side), jnp.bfloat16),
            pltpu.VMEM((waves, 2 * fp, tiles * 2 * side), jnp.bfloat16),
            pltpu.VMEM((owners, SHARD_ROWS, width), jnp.bfloat16),
            pltpu.VMEM((n, SHARD_ROWS, width), jnp.bfloat16),
            pltpu.VMEM((owners, SHARD_ROWS, width), jnp.bfloat16),
            pltpu.VMEM((owners, SHARD_ROWS // 2, LANES), jnp.float32),
            pltpu.VMEM((tiles, side_u, side), jnp.bfloat16),
            pltpu.VMEM((tiles, side_u, side), jnp.bfloat16),
            pltpu.VMEM((tiles, side_u, side), jnp.float32),
            pltpu.VMEM(turned, jnp.bfloat16),
            pltpu.VMEM(turned, jnp.bfloat16),
            dma((owners,)), dma((n,)),
            dma((n,)), dma((owners,)),
            dma((n,)), dma((owners,)),
            dma((tiles,)), dma((tiles,)),
            dma((n,)), dma((n,)),
        ],
        compiler_params=pltpu.CompilerParams(
            collective_id=0, has_side_effects=True, vmem_limit_bytes=64 << 20
        ),
    )(field, active_rows, kern, target)


def solution(mesh):
    placed = (
        P("wa", "cand", None, "gx", None, "gy", None),
        P("gx", None),
        P("wa", None, None, None, None),
        P("wa", None, None),
    )
    return jax.shard_map(
        functools.partial(on_device, mesh.shape["gx"], mesh.shape["gy"]),
        mesh=mesh,
        in_specs=placed,
        out_specs=(P("gx", "cand", "gy", None), P("wa", "cand", None)),
        check_vma=False,
    )
```

```python
import functools

import jax
import jax.numpy as jnp
from jax import lax
from jax.experimental import pallas as pl
from jax.experimental.pallas import tpu as pltpu
from jax.sharding import PartitionSpec as P

MESH = pl.DeviceIdType.MESH
SHARD_ROWS = 16
LANES = 128


def each(count, body):
    if count <= 16:
        for step in range(count):
            body(step)
    else:
        lax.fori_loop(0, count, lambda step, carry: (body(step), carry)[1], 0)


def times_i(value):
    parts = []
    for first in range(0, value.shape[1], LANES):
        part = pltpu.roll(value[:, first : first + LANES], LANES // 2, 1)
        lane = lax.broadcasted_iota(jnp.int32, part.shape, 1)
        parts.append(jnp.where(lane < LANES // 2, -part, part))
    return jnp.concatenate(parts, axis=1)


def kernel(
    nx, ny, field_far, rows, kern_far, target_far, grad, inten,
    field, kern, target, field_in, kern_in, target_in, plane, weights, fpart, frecv, src, ibuf, pown, ppeer, total, tsend, trecv,
    rs_send, rs_recv, ag_send, ag_recv, in_send, in_recv, wa_send, wa_recv, tr_send, tr_recv,
):
    n = nx * ny
    gx, gy, wa = lax.axis_index("gx"), lax.axis_index("gy"), lax.axis_index("wa")
    me = gx * ny + gy
    waves, pols, _, _, tiles, side_u, side = field.shape
    fp = kern.shape[3]
    loads = []
    for l in range(waves):
        loads.append(
            (
                pltpu.make_async_copy(kern_far.at[l], kern.at[l], kern_in.at[l]),
                pltpu.make_async_copy(field_far.at[l], field.at[l], field_in.at[l]),
            )
        )
        for copy in loads[l]:
            copy.start()
    goals = pltpu.make_async_copy(target_far, target, target_in)
    goals.start()
    per_wave = fp // SHARD_ROWS
    owners = waves * per_wave
    group = side // side_u

    def peer_of(step):
        return lax.rem(me + step + 1, n)

    def place(peer):
        return {"gx": peer // ny, "gy": lax.rem(peer, ny)}

    barrier = pltpu.get_barrier_semaphore()

    def greet(step):
        pl.semaphore_signal(barrier, inc=1, device_id=place(peer_of(step)), device_id_type=MESH)

    each(n - 1, greet)
    pl.semaphore_signal(barrier, inc=1, device_id={"wa": 1 - wa}, device_id_type=MESH)

    def shard_copy(owner, slot):
        return pltpu.make_async_remote_copy(
            src_ref=fpart.at[owner], dst_ref=frecv.at[slot],
            send_sem=rs_send.at[owner], recv_sem=rs_recv.at[slot],
            device_id=place(owner), device_id_type=MESH,
        )

    row_index = lax.broadcasted_iota(jnp.int32, (side_u, side), 0) + gy * side_u
    for l in range(waves):
        for copy in loads[l]:
            copy.wait()
        for j in range(tiles):
            real, imag = kern[l, 0, j], kern[l, 1, j]
            at = 2 * side * j
            weights[l, :fp, at : at + side] = real
            weights[l, :fp, at + side : at + 2 * side] = -imag
            weights[l, fp:, at : at + side] = imag
            weights[l, fp:, at + side : at + 2 * side] = real
            live = row_index < rows[0, j]
            for s in range(pols):
                for c in range(2):
                    value = field[l, s, c, 0, j].astype(jnp.float32)
                    plane[l, s * side_u : (s + 1) * side_u, at + c * side : at + (c + 1) * side] = jnp.where(
                        live, value, 0.0
                    ).astype(jnp.bfloat16)
        inner = lax.dot_general(
            plane[l], weights[l], (((1,), (1,)), ((), ())), preferred_element_type=jnp.float32
        )
        inner = jnp.concatenate(
            [inner[s * side_u : (s + 1) * side_u] for s in range(pols)], axis=1
        )
        both = []
        for value in (inner, times_i(inner)):
            both += [jnp.where(gy == k, value, 0.0) for k in range(group)]
        both = jnp.concatenate(both, axis=0)
        high = both.astype(jnp.bfloat16)
        low = (both - high.astype(jnp.float32)).astype(jnp.bfloat16)
        own = jnp.concatenate([kern[l, 0, gx], kern[l, 1, gx]], axis=1)
        focal = jnp.dot(own, high, preferred_element_type=jnp.float32) + jnp.dot(
            own, low, preferred_element_type=jnp.float32
        )
        for k in range(per_wave):
            fpart[l * per_wave + k] = focal[k * SHARD_ROWS : (k + 1) * SHARD_ROWS].astype(
                jnp.bfloat16
            )
        if l == 0:
            pl.semaphore_wait(barrier, n)
        for k in range(per_wave):
            owner = l * per_wave + lax.rem(me + k, per_wave)

            @pl.when(owner != me)
            def _():
                shard_copy(owner, me).start()

    goals.wait()

    def source_copy(peer, slot):
        return pltpu.make_async_remote_copy(
            src_ref=src.at[slot], dst_ref=src.at[slot],
            send_sem=ag_send.at[peer], recv_sem=ag_recv.at[slot],
            device_id=place(peer), device_id_type=MESH,
        )

    def intensity_copy(peer, slot):
        return pltpu.make_async_remote_copy(
            src_ref=ibuf.at[slot], dst_ref=ibuf.at[slot],
            send_sem=in_send.at[peer], recv_sem=in_recv.at[slot],
            device_id=place(peer), device_id_type=MESH,
        )

    def owned():
        frecv[me] = fpart[me]

        def arrive(step):
            shard_copy(me, peer_of(step)).wait_recv()

        each(n - 1, arrive)
        if n <= 16:
            focal = frecv[0].astype(jnp.float32)
            for slot in range(1, n):
                focal = focal + frecv[slot].astype(jnp.float32)
        else:
            focal = lax.fori_loop(
                1, n, lambda slot, value: value + frecv[slot].astype(jnp.float32),
                frecv[0].astype(jnp.float32),
            )
        square = focal * focal
        bright = square[:, :LANES]
        for s in range(1, pols):
            bright = bright + square[:, s * LANES : (s + 1) * LANES]
        bright = bright + pltpu.roll(bright, LANES // 2, 1)
        first = pl.multiple_of(lax.rem(me, per_wave) * SHARD_ROWS, SHARD_ROWS)
        goal = target[me // per_wave, pl.ds(first, SHARD_ROWS), :]
        excess = bright - jnp.concatenate([goal, goal], axis=1)
        src[me] = (focal * jnp.concatenate([excess] * pols, axis=1)).astype(jnp.bfloat16)
        each(n - 1, lambda step: source_copy(peer_of(step), me).start())
        half = SHARD_ROWS // 2
        lane = lax.broadcasted_iota(jnp.int32, (half, LANES), 1)
        ibuf[me] = jnp.where(lane < LANES // 2, bright[:half], bright[half:])
        each(n - 1, lambda step: intensity_copy(peer_of(step), me).start())

    if n > owners:
        pl.when(me < owners)(owned)
    else:
        owned()

    def swap(tile):
        return pltpu.make_async_remote_copy(
            src_ref=pown.at[tile], dst_ref=ppeer.at[tile],
            send_sem=wa_send.at[tile], recv_sem=wa_recv.at[tile],
            device_id={"wa": 1 - wa}, device_id_type=MESH,
        )

    for l in range(waves):
        for k in range(per_wave):
            owner = l * per_wave + k

            @pl.when(owner != me)
            def _():
                source_copy(owner, owner).wait_recv()

        source = src[l * per_wave : (l + 1) * per_wave].reshape(fp, pols * LANES)
        turned = (-times_i(source.astype(jnp.float32))).astype(jnp.bfloat16)
        own = kern[l, :, gx].reshape(2 * fp, side)
        side_rows = lax.dot_general(
            own, jnp.concatenate([source, turned], axis=0), (((0,), (0,)), ((), ())),
            preferred_element_type=jnp.float32,
        )
        picked = side_rows[:side_u]
        for k in range(1, group):
            picked = jnp.where(gy == k, side_rows[k * side_u : (k + 1) * side_u], picked)
        picked = jnp.concatenate(
            [picked[:, s * LANES : (s + 1) * LANES] for s in range(pols)], axis=0
        ).astype(jnp.bfloat16)
        for j in range(tiles):
            at = 2 * side * j
            back = jnp.dot(
                picked, weights[l, :, at : at + 2 * side], preferred_element_type=jnp.float32
            )
            terms = back * plane[l, :, at : at + 2 * side].astype(jnp.float32)
            terms = terms[:, :side] + terms[:, side:]
            value = terms[:side_u]
            for s in range(1, pols):
                value = value + terms[s * side_u : (s + 1) * side_u]
            if l > 0:
                value = value + total[j]
            if l < waves - 1:
                total[j] = value
            else:
                pown[j] = (value * jnp.float32(tiles * side / fp)).astype(jnp.bfloat16)
                swap(j).start()

    packs = tsend.shape[2] // side_u
    short = side_u // packs

    def turned_copy(peer, slot):
        return pltpu.make_async_remote_copy(
            src_ref=tsend.at[peer], dst_ref=trecv.at[slot],
            send_sem=tr_send.at[peer], recv_sem=tr_recv.at[slot],
            device_id=place(peer), device_id_type=MESH,
        )

    def turn(step):
        tile = lax.rem(gx + 1 + step, tiles)
        swap(tile).wait_recv()
        value = pown[tile].astype(jnp.float32) + ppeer[tile].astype(jnp.float32)
        total[tile] = value
        turned = value.T
        for k in range(ny):
            block = turned[k * side_u : (k + 1) * side_u]
            block = jnp.concatenate(
                [block[g * short : (g + 1) * short] for g in range(packs)], axis=1
            )
            peer = tile * ny + k
            tsend[peer] = block.astype(jnp.bfloat16)

            @pl.when(peer != me)
            def _():
                turned_copy(peer, me).start()

    each(tiles, turn)

    for owner in range(owners):
        @pl.when(owner != me)
        def _():
            intensity_copy(owner, owner).wait_recv()

        l, first, half = owner // per_wave, owner % per_wave * SHARD_ROWS, SHARD_ROWS // 2
        value = ibuf[owner]
        inten[l, first : first + half, :] = value[:, : LANES // 2]
        inten[l, first + half : first + 2 * half, :] = value[:, LANES // 2 :]

    trecv[me] = tsend[me]
    each(n - 1, lambda step: turned_copy(me, peer_of(step)).wait_recv())
    for j in range(tiles):
        blocks = [trecv[j * ny + k].astype(jnp.float32) for k in range(ny)]
        lines = [
            jnp.concatenate([block[:, g * side_u : (g + 1) * side_u] for block in blocks], axis=1)
            for g in range(packs)
        ]
        grad[0, j] = 0.5 * (total[j] + jnp.concatenate(lines, axis=0))

    each(tiles, lambda tile: swap(tile).wait_send())
    for owner in range(owners):
        @pl.when(owner != me)
        def _():
            shard_copy(owner, me).wait_send()

    def drain_owned():
        each(n - 1, lambda step: source_copy(peer_of(step), me).wait_send())
        each(n - 1, lambda step: intensity_copy(peer_of(step), me).wait_send())

    if n > owners:
        pl.when(me < owners)(drain_owned)
    else:
        drain_owned()
    each(n - 1, lambda step: turned_copy(peer_of(step), me).wait_send())


def deliver(grad, inten, grad_out, inten_out, grad_sems, inten_sems):
    copies = [
        pltpu.make_async_copy(grad.at[0, j], grad_out.at[0, j], grad_sems.at[j])
        for j in range(grad.shape[1])
    ] + [
        pltpu.make_async_copy(inten.at[l], inten_out.at[l], inten_sems.at[l])
        for l in range(inten.shape[0])
    ]
    for copy in copies:
        copy.start()
    for copy in copies:
        copy.wait()


def on_device(nx, ny, field, active_rows, kern, target):
    waves, pols, _, _, tiles, side_u, side = field.shape
    fp = kern.shape[3]
    n = nx * ny
    owners = waves * (fp // SHARD_ROWS)
    packs = LANES // side_u
    if (side_u // packs) % 16:
        packs = 1
    turned = (n, side_u // packs, side_u * packs)
    dma = pltpu.SemaphoreType.DMA
    vmem = pl.BlockSpec(memory_space=pltpu.VMEM)
    far = pl.BlockSpec(memory_space=pltpu.HBM)
    width = pols * LANES
    results = (
        jax.ShapeDtypeStruct((1, tiles, side_u, side), jnp.float32),
        jax.ShapeDtypeStruct((waves, fp, fp), jnp.float32),
    )
    grad, inten = pl.pallas_call(
        functools.partial(kernel, nx, ny),
        out_shape=results,
        in_specs=[far, pl.BlockSpec(memory_space=pltpu.SMEM), far, far],
        out_specs=(vmem, vmem),
        scratch_shapes=[
            pltpu.VMEM(field.shape, field.dtype),
            pltpu.VMEM(kern.shape, kern.dtype),
            pltpu.VMEM(target.shape, target.dtype),
            dma((waves,)), dma((waves,)), dma,
            pltpu.VMEM((waves, pols * side_u, tiles * 2 * side), jnp.bfloat16),
            pltpu.VMEM((waves, 2 * fp, tiles * 2 * side), jnp.bfloat16),
            pltpu.VMEM((owners, SHARD_ROWS, width), jnp.bfloat16),
            pltpu.VMEM((n, SHARD_ROWS, width), jnp.bfloat16),
            pltpu.VMEM((owners, SHARD_ROWS, width), jnp.bfloat16),
            pltpu.VMEM((owners, SHARD_ROWS // 2, LANES), jnp.float32),
            pltpu.VMEM((tiles, side_u, side), jnp.bfloat16),
            pltpu.VMEM((tiles, side_u, side), jnp.bfloat16),
            pltpu.VMEM((tiles, side_u, side), jnp.float32),
            pltpu.VMEM(turned, jnp.bfloat16),
            pltpu.VMEM(turned, jnp.bfloat16),
            dma((owners,)), dma((n,)),
            dma((n,)), dma((owners,)),
            dma((n,)), dma((owners,)),
            dma((tiles,)), dma((tiles,)),
            dma((n,)), dma((n,)),
        ],
        compiler_params=pltpu.CompilerParams(
            collective_id=0, has_side_effects=True, vmem_limit_bytes=64 << 20
        ),
    )(field, active_rows, kern, target)
    return pl.pallas_call(
        deliver,
        out_shape=results,
        in_specs=[far, far],
        out_specs=(far, far),
        scratch_shapes=[dma((tiles,)), dma((waves,))],
        compiler_params=pltpu.CompilerParams(vmem_limit_bytes=64 << 20),
    )(grad, inten)


def solution(mesh):
    placed = (
        P("wa", "cand", None, "gx", None, "gy", None),
        P("gx", None),
        P("wa", None, None, None, None),
        P("wa", None, None),
    )
    return jax.shard_map(
        functools.partial(on_device, mesh.shape["gx"], mesh.shape["gy"]),
        mesh=mesh,
        in_specs=placed,
        out_specs=(P("gx", "cand", "gy", None), P("wa", "cand", None)),
        check_vma=False,
    )
```

```python
import functools

import jax
import jax.numpy as jnp
from jax import lax
from jax.experimental import pallas as pl
from jax.experimental.pallas import tpu as pltpu
from jax.sharding import PartitionSpec as P

MESH = pl.DeviceIdType.MESH
SHARD_ROWS = 16
LANES = 128


def each(count, body):
    if count <= 16:
        for step in range(count):
            body(step)
    else:
        lax.fori_loop(0, count, lambda step, carry: (body(step), carry)[1], 0)


def times_i(value):
    parts = []
    for first in range(0, value.shape[1], LANES):
        part = pltpu.roll(value[:, first : first + LANES], LANES // 2, 1)
        lane = lax.broadcasted_iota(jnp.int32, part.shape, 1)
        parts.append(jnp.where(lane < LANES // 2, -part, part))
    return jnp.concatenate(parts, axis=1)


def kernel(
    nx, ny, field_far, rows, kern_far, target_far, grad_far, inten_far,
    grad, inten, grad_out, inten_out, field, kern, target, field_in, kern_in, target_in, plane, weights, fpart, frecv, src, ibuf, pown, ppeer, total, tsend, trecv,
    rs_send, rs_recv, ag_send, ag_recv, in_send, in_recv, wa_send, wa_recv, tr_send, tr_recv,
):
    n = nx * ny
    gx, gy, wa = lax.axis_index("gx"), lax.axis_index("gy"), lax.axis_index("wa")
    me = gx * ny + gy
    waves, pols, _, _, tiles, side_u, side = field.shape
    fp = kern.shape[3]
    loads = []
    for l in range(waves):
        loads.append(
            (
                pltpu.make_async_copy(kern_far.at[l], kern.at[l], kern_in.at[l]),
                pltpu.make_async_copy(field_far.at[l], field.at[l], field_in.at[l]),
            )
        )
        for copy in loads[l]:
            copy.start()
    goals = pltpu.make_async_copy(target_far, target, target_in)
    goals.start()
    per_wave = fp // SHARD_ROWS
    owners = waves * per_wave
    group = side // side_u

    def peer_of(step):
        return lax.rem(me + step + 1, n)

    def place(peer):
        return {"gx": peer // ny, "gy": lax.rem(peer, ny)}

    barrier = pltpu.get_barrier_semaphore()

    def greet(step):
        pl.semaphore_signal(barrier, inc=1, device_id=place(peer_of(step)), device_id_type=MESH)

    each(n - 1, greet)
    pl.semaphore_signal(barrier, inc=1, device_id={"wa": 1 - wa}, device_id_type=MESH)

    def shard_copy(owner, slot):
        return pltpu.make_async_remote_copy(
            src_ref=fpart.at[owner], dst_ref=frecv.at[slot],
            send_sem=rs_send.at[owner], recv_sem=rs_recv.at[slot],
            device_id=place(owner), device_id_type=MESH,
        )

    row_index = lax.broadcasted_iota(jnp.int32, (side_u, side), 0) + gy * side_u
    for l in range(waves):
        for copy in loads[l]:
            copy.wait()
        for j in range(tiles):
            real, imag = kern[l, 0, j], kern[l, 1, j]
            at = 2 * side * j
            weights[l, :fp, at : at + side] = real
            weights[l, :fp, at + side : at + 2 * side] = -imag
            weights[l, fp:, at : at + side] = imag
            weights[l, fp:, at + side : at + 2 * side] = real
            live = row_index < rows[0, j]
            for s in range(pols):
                for c in range(2):
                    value = field[l, s, c, 0, j].astype(jnp.float32)
                    plane[l, s * side_u : (s + 1) * side_u, at + c * side : at + (c + 1) * side] = jnp.where(
                        live, value, 0.0
                    ).astype(jnp.bfloat16)
        inner = lax.dot_general(
            plane[l], weights[l], (((1,), (1,)), ((), ())), preferred_element_type=jnp.float32
        )
        inner = jnp.concatenate(
            [inner[s * side_u : (s + 1) * side_u] for s in range(pols)], axis=1
        )
        both = []
        for value in (inner, times_i(inner)):
            both += [jnp.where(gy == k, value, 0.0) for k in range(group)]
        both = jnp.concatenate(both, axis=0)
        high = both.astype(jnp.bfloat16)
        low = (both - high.astype(jnp.float32)).astype(jnp.bfloat16)
        own = jnp.concatenate([kern[l, 0, gx], kern[l, 1, gx]], axis=1)
        focal = jnp.dot(own, high, preferred_element_type=jnp.float32) + jnp.dot(
            own, low, preferred_element_type=jnp.float32
        )
        for k in range(per_wave):
            fpart[l * per_wave + k] = focal[k * SHARD_ROWS : (k + 1) * SHARD_ROWS].astype(
                jnp.bfloat16
            )
        if l == 0:
            pl.semaphore_wait(barrier, n)
        for k in range(per_wave):
            owner = l * per_wave + lax.rem(me + k, per_wave)

            @pl.when(owner != me)
            def _():
                shard_copy(owner, me).start()

    goals.wait()

    def source_copy(peer, slot):
        return pltpu.make_async_remote_copy(
            src_ref=src.at[slot], dst_ref=src.at[slot],
            send_sem=ag_send.at[peer], recv_sem=ag_recv.at[slot],
            device_id=place(peer), device_id_type=MESH,
        )

    def intensity_copy(peer, slot):
        return pltpu.make_async_remote_copy(
            src_ref=ibuf.at[slot], dst_ref=ibuf.at[slot],
            send_sem=in_send.at[peer], recv_sem=in_recv.at[slot],
            device_id=place(peer), device_id_type=MESH,
        )

    def owned():
        frecv[me] = fpart[me]

        def arrive(step):
            shard_copy(me, peer_of(step)).wait_recv()

        each(n - 1, arrive)
        if n <= 16:
            focal = frecv[0].astype(jnp.float32)
            for slot in range(1, n):
                focal = focal + frecv[slot].astype(jnp.float32)
        else:
            focal = lax.fori_loop(
                1, n, lambda slot, value: value + frecv[slot].astype(jnp.float32),
                frecv[0].astype(jnp.float32),
            )
        square = focal * focal
        bright = square[:, :LANES]
        for s in range(1, pols):
            bright = bright + square[:, s * LANES : (s + 1) * LANES]
        bright = bright + pltpu.roll(bright, LANES // 2, 1)
        first = pl.multiple_of(lax.rem(me, per_wave) * SHARD_ROWS, SHARD_ROWS)
        goal = target[me // per_wave, pl.ds(first, SHARD_ROWS), :]
        excess = bright - jnp.concatenate([goal, goal], axis=1)
        src[me] = (focal * jnp.concatenate([excess] * pols, axis=1)).astype(jnp.bfloat16)
        each(n - 1, lambda step: source_copy(peer_of(step), me).start())
        half = SHARD_ROWS // 2
        lane = lax.broadcasted_iota(jnp.int32, (half, LANES), 1)
        ibuf[me] = jnp.where(lane < LANES // 2, bright[:half], bright[half:])
        each(n - 1, lambda step: intensity_copy(peer_of(step), me).start())

    if n > owners:
        pl.when(me < owners)(owned)
    else:
        owned()

    def swap(tile):
        return pltpu.make_async_remote_copy(
            src_ref=pown.at[tile], dst_ref=ppeer.at[tile],
            send_sem=wa_send.at[tile], recv_sem=wa_recv.at[tile],
            device_id={"wa": 1 - wa}, device_id_type=MESH,
        )

    for l in range(waves):
        for k in range(per_wave):
            owner = l * per_wave + k

            @pl.when(owner != me)
            def _():
                source_copy(owner, owner).wait_recv()

        source = src[l * per_wave : (l + 1) * per_wave].reshape(fp, pols * LANES)
        turned = (-times_i(source.astype(jnp.float32))).astype(jnp.bfloat16)
        own = kern[l, :, gx].reshape(2 * fp, side)
        side_rows = lax.dot_general(
            own, jnp.concatenate([source, turned], axis=0), (((0,), (0,)), ((), ())),
            preferred_element_type=jnp.float32,
        )
        picked = side_rows[:side_u]
        for k in range(1, group):
            picked = jnp.where(gy == k, side_rows[k * side_u : (k + 1) * side_u], picked)
        picked = jnp.concatenate(
            [picked[:, s * LANES : (s + 1) * LANES] for s in range(pols)], axis=0
        ).astype(jnp.bfloat16)
        for j in range(tiles):
            at = 2 * side * j
            back = jnp.dot(
                picked, weights[l, :, at : at + 2 * side], preferred_element_type=jnp.float32
            )
            terms = back * plane[l, :, at : at + 2 * side].astype(jnp.float32)
            terms = terms[:, :side] + terms[:, side:]
            value = terms[:side_u]
            for s in range(1, pols):
                value = value + terms[s * side_u : (s + 1) * side_u]
            if l > 0:
                value = value + total[j]
            if l < waves - 1:
                total[j] = value
            else:
                pown[j] = (value * jnp.float32(tiles * side / fp)).astype(jnp.bfloat16)
                swap(j).start()

    packs = tsend.shape[2] // side_u
    short = side_u // packs

    def turned_copy(peer, slot):
        return pltpu.make_async_remote_copy(
            src_ref=tsend.at[peer], dst_ref=trecv.at[slot],
            send_sem=tr_send.at[peer], recv_sem=tr_recv.at[slot],
            device_id=place(peer), device_id_type=MESH,
        )

    def turn(step):
        tile = lax.rem(gx + 1 + step, tiles)
        swap(tile).wait_recv()
        value = pown[tile].astype(jnp.float32) + ppeer[tile].astype(jnp.float32)
        total[tile] = value
        turned = value.T
        for k in range(ny):
            block = turned[k * side_u : (k + 1) * side_u]
            block = jnp.concatenate(
                [block[g * short : (g + 1) * short] for g in range(packs)], axis=1
            )
            peer = tile * ny + k
            tsend[peer] = block.astype(jnp.bfloat16)

            @pl.when(peer != me)
            def _():
                turned_copy(peer, me).start()

    each(tiles, turn)

    for owner in range(owners):
        @pl.when(owner != me)
        def _():
            intensity_copy(owner, owner).wait_recv()

        l, first, half = owner // per_wave, owner % per_wave * SHARD_ROWS, SHARD_ROWS // 2
        value = ibuf[owner]
        inten[l, first : first + half, :] = value[:, : LANES // 2]
        inten[l, first + half : first + 2 * half, :] = value[:, LANES // 2 :]

    inten_done = pltpu.make_async_copy(inten, inten_far, inten_out)
    inten_done.start()

    def grad_done(tile):
        return pltpu.make_async_copy(grad.at[tile], grad_far.at[0, tile], grad_out.at[tile])

    trecv[me] = tsend[me]

    def finish(step):
        tile = lax.rem(gx + step, tiles)
        for k in range(ny):
            peer = tile * ny + k

            @pl.when(peer != me)
            def _():
                turned_copy(me, peer).wait_recv()

        blocks = [trecv[tile * ny + k].astype(jnp.float32) for k in range(ny)]
        lines = [
            jnp.concatenate([block[:, g * side_u : (g + 1) * side_u] for block in blocks], axis=1)
            for g in range(packs)
        ]
        grad[tile] = 0.5 * (total[tile] + jnp.concatenate(lines, axis=0))
        grad_done(tile).start()

    each(tiles, finish)

    each(tiles, lambda tile: swap(tile).wait_send())
    for owner in range(owners):
        @pl.when(owner != me)
        def _():
            shard_copy(owner, me).wait_send()

    def drain_owned():
        each(n - 1, lambda step: source_copy(peer_of(step), me).wait_send())
        each(n - 1, lambda step: intensity_copy(peer_of(step), me).wait_send())

    if n > owners:
        pl.when(me < owners)(drain_owned)
    else:
        drain_owned()
    each(n - 1, lambda step: turned_copy(peer_of(step), me).wait_send())
    inten_done.wait()
    each(tiles, lambda tile: grad_done(tile).wait())


def on_device(nx, ny, field, active_rows, kern, target):
    waves, pols, _, _, tiles, side_u, side = field.shape
    fp = kern.shape[3]
    n = nx * ny
    owners = waves * (fp // SHARD_ROWS)
    packs = LANES // side_u
    if (side_u // packs) % 16:
        packs = 1
    turned = (n, side_u // packs, side_u * packs)
    dma = pltpu.SemaphoreType.DMA
    far = pl.BlockSpec(memory_space=pltpu.HBM)
    width = pols * LANES
    return pl.pallas_call(
        functools.partial(kernel, nx, ny),
        out_shape=(
            jax.ShapeDtypeStruct((1, tiles, side_u, side), jnp.float32),
            jax.ShapeDtypeStruct((waves, fp, fp), jnp.float32),
        ),
        in_specs=[far, pl.BlockSpec(memory_space=pltpu.SMEM), far, far],
        out_specs=(far, far),
        scratch_shapes=[
            pltpu.VMEM((tiles, side_u, side), jnp.float32),
            pltpu.VMEM((waves, fp, fp), jnp.float32),
            dma((tiles,)), dma,
            pltpu.VMEM(field.shape, field.dtype),
            pltpu.VMEM(kern.shape, kern.dtype),
            pltpu.VMEM(target.shape, target.dtype),
            dma((waves,)), dma((waves,)), dma,
            pltpu.VMEM((waves, pols * side_u, tiles * 2 * side), jnp.bfloat16),
            pltpu.VMEM((waves, 2 * fp, tiles * 2 * side), jnp.bfloat16),
            pltpu.VMEM((owners, SHARD_ROWS, width), jnp.bfloat16),
            pltpu.VMEM((n, SHARD_ROWS, width), jnp.bfloat16),
            pltpu.VMEM((owners, SHARD_ROWS, width), jnp.bfloat16),
            pltpu.VMEM((owners, SHARD_ROWS // 2, LANES), jnp.float32),
            pltpu.VMEM((tiles, side_u, side), jnp.bfloat16),
            pltpu.VMEM((tiles, side_u, side), jnp.bfloat16),
            pltpu.VMEM((tiles, side_u, side), jnp.float32),
            pltpu.VMEM(turned, jnp.bfloat16),
            pltpu.VMEM(turned, jnp.bfloat16),
            dma((owners,)), dma((n,)),
            dma((n,)), dma((owners,)),
            dma((n,)), dma((owners,)),
            dma((tiles,)), dma((tiles,)),
            dma((n,)), dma((n,)),
        ],
        compiler_params=pltpu.CompilerParams(
            collective_id=0, has_side_effects=True, vmem_limit_bytes=64 << 20
        ),
    )(field, active_rows, kern, target)


def solution(mesh):
    placed = (
        P("wa", "cand", None, "gx", None, "gy", None),
        P("gx", None),
        P("wa", None, None, None, None),
        P("wa", None, None),
    )
    return jax.shard_map(
        functools.partial(on_device, mesh.shape["gx"], mesh.shape["gy"]),
        mesh=mesh,
        in_specs=placed,
        out_specs=(P("gx", "cand", "gy", None), P("wa", "cand", None)),
        check_vma=False,
    )
```

```python
import functools

import jax
import jax.numpy as jnp
from jax import lax
from jax.experimental import pallas as pl
from jax.experimental.pallas import tpu as pltpu
from jax.sharding import PartitionSpec as P

MESH = pl.DeviceIdType.MESH
SHARD_ROWS = 16
LANES = 128


def each(count, body):
    if count <= 16:
        for step in range(count):
            body(step)
    else:
        lax.fori_loop(0, count, lambda step, carry: (body(step), carry)[1], 0)


def times_i(value):
    parts = []
    for first in range(0, value.shape[1], LANES):
        part = pltpu.roll(value[:, first : first + LANES], LANES // 2, 1)
        lane = lax.broadcasted_iota(jnp.int32, part.shape, 1)
        parts.append(jnp.where(lane < LANES // 2, -part, part))
    return jnp.concatenate(parts, axis=1)


def kernel(
    nx, ny, field_far, rows, kern_far, target_far, grad, inten,
    field, kern, target, field_in, kern_in, target_in, plane, weights, fpart, frecv, src, ibuf, pown, ppeer, total, tsend, trecv,
    rs_send, rs_recv, ag_send, ag_recv, in_send, in_recv, wa_send, wa_recv, tr_send, tr_recv,
):
    n = nx * ny
    gx, gy, wa = lax.axis_index("gx"), lax.axis_index("gy"), lax.axis_index("wa")
    me = gx * ny + gy
    waves, pols, _, _, tiles, side_u, side = field.shape
    fp = kern.shape[3]
    loads = []
    for l in range(waves):
        loads.append(
            (
                pltpu.make_async_copy(kern_far.at[l], kern.at[l], kern_in.at[l]),
                pltpu.make_async_copy(field_far.at[l], field.at[l], field_in.at[l]),
            )
        )
        for copy in loads[l]:
            copy.start()
    goals = pltpu.make_async_copy(target_far, target, target_in)
    goals.start()
    per_wave = fp // SHARD_ROWS
    owners = waves * per_wave
    group = side // side_u

    def peer_of(step):
        return lax.rem(me + step + 1, n)

    def place(peer):
        return {"gx": peer // ny, "gy": lax.rem(peer, ny)}

    barrier = pltpu.get_barrier_semaphore()

    def greet(step):
        pl.semaphore_signal(barrier, inc=1, device_id=place(peer_of(step)), device_id_type=MESH)

    each(n - 1, greet)
    pl.semaphore_signal(barrier, inc=1, device_id={"wa": 1 - wa}, device_id_type=MESH)

    def shard_copy(owner, slot):
        return pltpu.make_async_remote_copy(
            src_ref=fpart.at[owner], dst_ref=frecv.at[slot],
            send_sem=rs_send.at[owner], recv_sem=rs_recv.at[slot],
            device_id=place(owner), device_id_type=MESH,
        )

    row_index = lax.broadcasted_iota(jnp.int32, (side_u, side), 0) + gy * side_u
    for l in range(waves):
        for copy in loads[l]:
            copy.wait()
        for j in range(tiles):
            real, imag = kern[l, 0, j], kern[l, 1, j]
            at = 2 * side * j
            weights[l, :fp, at : at + side] = real
            weights[l, :fp, at + side : at + 2 * side] = -imag
            weights[l, fp:, at : at + side] = imag
            weights[l, fp:, at + side : at + 2 * side] = real
            live = row_index < rows[0, j]
            for s in range(pols):
                for c in range(2):
                    value = field[l, s, c, 0, j].astype(jnp.float32)
                    plane[l, s * side_u : (s + 1) * side_u, at + c * side : at + (c + 1) * side] = jnp.where(
                        live, value, 0.0
                    ).astype(jnp.bfloat16)
        inner = lax.dot_general(
            plane[l], weights[l], (((1,), (1,)), ((), ())), preferred_element_type=jnp.float32
        )
        inner = jnp.concatenate(
            [inner[s * side_u : (s + 1) * side_u] for s in range(pols)], axis=1
        )
        both = []
        for value in (inner, times_i(inner)):
            both += [jnp.where(gy == k, value, 0.0) for k in range(group)]
        both = jnp.concatenate(both, axis=0)
        high = both.astype(jnp.bfloat16)
        low = (both - high.astype(jnp.float32)).astype(jnp.bfloat16)
        own = jnp.concatenate([kern[l, 0, gx], kern[l, 1, gx]], axis=1)
        focal = jnp.dot(own, high, preferred_element_type=jnp.float32) + jnp.dot(
            own, low, preferred_element_type=jnp.float32
        )
        for k in range(per_wave):
            fpart[l * per_wave + k] = focal[k * SHARD_ROWS : (k + 1) * SHARD_ROWS].astype(
                jnp.bfloat16
            )
        if l == 0:
            pl.semaphore_wait(barrier, n)
        for k in range(per_wave):
            owner = l * per_wave + lax.rem(me + k, per_wave)

            @pl.when(owner != me)
            def _():
                shard_copy(owner, me).start()

    goals.wait()

    def source_copy(peer, slot):
        return pltpu.make_async_remote_copy(
            src_ref=src.at[slot], dst_ref=src.at[slot],
            send_sem=ag_send.at[peer], recv_sem=ag_recv.at[slot],
            device_id=place(peer), device_id_type=MESH,
        )

    def intensity_copy(peer, slot):
        return pltpu.make_async_remote_copy(
            src_ref=ibuf.at[slot], dst_ref=ibuf.at[slot],
            send_sem=in_send.at[peer], recv_sem=in_recv.at[slot],
            device_id=place(peer), device_id_type=MESH,
        )

    def owned():
        frecv[me] = fpart[me]

        def arrive(step):
            shard_copy(me, peer_of(step)).wait_recv()

        each(n - 1, arrive)
        if n <= 16:
            focal = frecv[0].astype(jnp.float32)
            for slot in range(1, n):
                focal = focal + frecv[slot].astype(jnp.float32)
        else:
            focal = lax.fori_loop(
                1, n, lambda slot, value: value + frecv[slot].astype(jnp.float32),
                frecv[0].astype(jnp.float32),
            )
        square = focal * focal
        bright = square[:, :LANES]
        for s in range(1, pols):
            bright = bright + square[:, s * LANES : (s + 1) * LANES]
        bright = bright + pltpu.roll(bright, LANES // 2, 1)
        first = pl.multiple_of(lax.rem(me, per_wave) * SHARD_ROWS, SHARD_ROWS)
        goal = target[me // per_wave, pl.ds(first, SHARD_ROWS), :]
        excess = bright - jnp.concatenate([goal, goal], axis=1)
        src[me] = (focal * jnp.concatenate([excess] * pols, axis=1)).astype(jnp.bfloat16)
        each(n - 1, lambda step: source_copy(peer_of(step), me).start())
        half = SHARD_ROWS // 2
        lane = lax.broadcasted_iota(jnp.int32, (half, LANES), 1)
        ibuf[me] = jnp.where(lane < LANES // 2, bright[:half], bright[half:])
        each(n - 1, lambda step: intensity_copy(peer_of(step), me).start())

    if n > owners:
        pl.when(me < owners)(owned)
    else:
        owned()

    def swap(tile):
        return pltpu.make_async_remote_copy(
            src_ref=pown.at[tile], dst_ref=ppeer.at[tile],
            send_sem=wa_send.at[tile], recv_sem=wa_recv.at[tile],
            device_id={"wa": 1 - wa}, device_id_type=MESH,
        )

    for l in range(waves):
        for k in range(per_wave):
            owner = l * per_wave + k

            @pl.when(owner != me)
            def _():
                source_copy(owner, owner).wait_recv()

        source = src[l * per_wave : (l + 1) * per_wave].reshape(fp, pols * LANES)
        turned = (-times_i(source.astype(jnp.float32))).astype(jnp.bfloat16)
        own = kern[l, :, gx].reshape(2 * fp, side)
        side_rows = lax.dot_general(
            own, jnp.concatenate([source, turned], axis=0), (((0,), (0,)), ((), ())),
            preferred_element_type=jnp.float32,
        )
        picked = side_rows[:side_u]
        for k in range(1, group):
            picked = jnp.where(gy == k, side_rows[k * side_u : (k + 1) * side_u], picked)
        picked = jnp.concatenate(
            [picked[:, s * LANES : (s + 1) * LANES] for s in range(pols)], axis=0
        ).astype(jnp.bfloat16)
        for j in range(tiles):
            at = 2 * side * j
            back = jnp.dot(
                picked, weights[l, :, at : at + 2 * side], preferred_element_type=jnp.float32
            )
            terms = back * plane[l, :, at : at + 2 * side].astype(jnp.float32)
            terms = terms[:, :side] + terms[:, side:]
            value = terms[:side_u]
            for s in range(1, pols):
                value = value + terms[s * side_u : (s + 1) * side_u]
            if l > 0:
                value = value + total[j]
            if l < waves - 1:
                total[j] = value
            else:
                pown[j] = (value * jnp.float32(tiles * side / fp)).astype(jnp.bfloat16)
                swap(j).start()

    packs = tsend.shape[2] // side_u
    short = side_u // packs

    def turned_copy(peer, slot):
        return pltpu.make_async_remote_copy(
            src_ref=tsend.at[peer], dst_ref=trecv.at[slot],
            send_sem=tr_send.at[peer], recv_sem=tr_recv.at[slot],
            device_id=place(peer), device_id_type=MESH,
        )

    def turn(step):
        tile = lax.rem(gx + 1 + step, tiles)
        swap(tile).wait_recv()
        value = pown[tile].astype(jnp.float32) + ppeer[tile].astype(jnp.float32)
        total[tile] = value
        turned = value.T
        for k in range(ny):
            block = turned[k * side_u : (k + 1) * side_u]
            block = jnp.concatenate(
                [block[g * short : (g + 1) * short] for g in range(packs)], axis=1
            )
            peer = tile * ny + k
            tsend[peer] = block.astype(jnp.bfloat16)

            @pl.when(peer != me)
            def _():
                turned_copy(peer, me).start()

    each(tiles, turn)

    for owner in range(owners):
        @pl.when(owner != me)
        def _():
            intensity_copy(owner, owner).wait_recv()

        l, first, half = owner // per_wave, owner % per_wave * SHARD_ROWS, SHARD_ROWS // 2
        value = ibuf[owner]
        inten[l, first : first + half, :] = value[:, : LANES // 2]
        inten[l, first + half : first + 2 * half, :] = value[:, LANES // 2 :]

    trecv[me] = tsend[me]
    each(n - 1, lambda step: turned_copy(me, peer_of(step)).wait_recv())
    for j in range(tiles):
        blocks = [trecv[j * ny + k].astype(jnp.float32) for k in range(ny)]
        lines = [
            jnp.concatenate([block[:, g * side_u : (g + 1) * side_u] for block in blocks], axis=1)
            for g in range(packs)
        ]
        grad[0, j] = 0.5 * (total[j] + jnp.concatenate(lines, axis=0))

    each(tiles, lambda tile: swap(tile).wait_send())
    for owner in range(owners):
        @pl.when(owner != me)
        def _():
            shard_copy(owner, me).wait_send()

    def drain_owned():
        each(n - 1, lambda step: source_copy(peer_of(step), me).wait_send())
        each(n - 1, lambda step: intensity_copy(peer_of(step), me).wait_send())

    if n > owners:
        pl.when(me < owners)(drain_owned)
    else:
        drain_owned()
    each(n - 1, lambda step: turned_copy(peer_of(step), me).wait_send())


def on_device(nx, ny, field, active_rows, kern, target):
    waves, pols, _, _, tiles, side_u, side = field.shape
    fp = kern.shape[3]
    n = nx * ny
    owners = waves * (fp // SHARD_ROWS)
    packs = LANES // side_u
    if (side_u // packs) % 16:
        packs = 1
    turned = (n, side_u // packs, side_u * packs)
    dma = pltpu.SemaphoreType.DMA
    vmem = pl.BlockSpec(memory_space=pltpu.VMEM)
    far = pl.BlockSpec(memory_space=pltpu.HBM)
    width = pols * LANES
    return pl.pallas_call(
        functools.partial(kernel, nx, ny),
        out_shape=(
            jax.ShapeDtypeStruct((1, tiles, side_u, side), jnp.float32),
            jax.ShapeDtypeStruct((waves, fp, fp), jnp.float32),
        ),
        in_specs=[far, pl.BlockSpec(memory_space=pltpu.SMEM), far, far],
        out_specs=(vmem, vmem),
        scratch_shapes=[
            pltpu.VMEM(field.shape, field.dtype),
            pltpu.VMEM(kern.shape, kern.dtype),
            pltpu.VMEM(target.shape, target.dtype),
            dma((waves,)), dma((waves,)), dma,
            pltpu.VMEM((waves, pols * side_u, tiles * 2 * side), jnp.bfloat16),
            pltpu.VMEM((waves, 2 * fp, tiles * 2 * side), jnp.bfloat16),
            pltpu.VMEM((owners, SHARD_ROWS, width), jnp.bfloat16),
            pltpu.VMEM((n, SHARD_ROWS, width), jnp.bfloat16),
            pltpu.VMEM((owners, SHARD_ROWS, width), jnp.bfloat16),
            pltpu.VMEM((owners, SHARD_ROWS // 2, LANES), jnp.float32),
            pltpu.VMEM((tiles, side_u, side), jnp.bfloat16),
            pltpu.VMEM((tiles, side_u, side), jnp.bfloat16),
            pltpu.VMEM((tiles, side_u, side), jnp.float32),
            pltpu.VMEM(turned, jnp.bfloat16),
            pltpu.VMEM(turned, jnp.bfloat16),
            dma((owners,)), dma((n,)),
            dma((n,)), dma((owners,)),
            dma((n,)), dma((owners,)),
            dma((tiles,)), dma((tiles,)),
            dma((n,)), dma((n,)),
        ],
        compiler_params=pltpu.CompilerParams(
            collective_id=0, has_side_effects=True, vmem_limit_bytes=54848 << 10
        ),
    )(field, active_rows, kern, target)


def solution(mesh):
    placed = (
        P("wa", "cand", None, "gx", None, "gy", None),
        P("gx", None),
        P("wa", None, None, None, None),
        P("wa", None, None),
    )
    return jax.shard_map(
        functools.partial(on_device, mesh.shape["gx"], mesh.shape["gy"]),
        mesh=mesh,
        in_specs=placed,
        out_specs=(P("gx", "cand", "gy", None), P("wa", "cand", None)),
        check_vma=False,
    )
```
